256 devices in a mesh: row: 64 (over z, x, core), rep: 4 (over y).
Axes of the slice: x: 4, y: 4, z: 8, core: 2. Of those that a mesh axis runs over, the one named last changes fastest.
Arguments:
- features: bfloat16 [65536, 128], P('row', 'rep'), may hold values from -6 to 6
- tiles: bfloat16 [512, 16, 128, 128], P('row'), may hold values from -0.1875 to 0.1875
- tile_cols: int32 [512, 16], P('row'), may hold values from 0 to 511, as said below
- counts: int32 [512], P('row'), may hold values from 1 to 16
- weight: bfloat16 [128, 256], P(None, 'rep'), may hold values from -0.5 to 0.5
- bias: float32 [256], P('rep'), may hold values from -3 to 3
- cotangent: bfloat16 [65536, 256], P('row', 'rep'), may hold values from -6 to 6
Outputs:
- hidden: bfloat16 [65536, 256], P('row', 'rep')
- grad_weight: float32 [128, 256], P(None, 'rep')
- grad_bias: float32 [256], P('rep')
- grad_features: bfloat16 [65536, 128], P('row', 'rep')
The draws below stay inside these ranges and needn't reach their ends.
Inputs may be any that keep to these rules, and one draw needn't show every extreme that they name: `tile_cols`: row block i lies on index i // 8 of row. Every slot of it names a column block lying on an index of row at most two away from that index (cyclically), or on the index half the axis away.
All inputs are finite; a program needn't handle non-finite values.
Results may differ from the reference program's by a relative error of at most 0.007.
Values may be sent and summed in bfloat16 or wider, within the bound.
A program may use at most 128 MiB of HBM per device.

```python
import jax
import jax.numpy as jnp
from jax import lax

FIN = 128
HID = 256
TILE = 128
CAP = 16
RB_DEV = 8
NRB = 512
NV = 65536


def draw_tile_cols(key, part):
    key = jax.random.fold_in(key, 11)
    keys = jax.random.split(key, 3)
    row_count = NRB // RB_DEV
    row_ids = jnp.arange(NRB, dtype=jnp.int32)[:, None]
    owner = row_ids // RB_DEV
    nearby = jax.random.randint(keys[0], (NRB, CAP), -2 * RB_DEV, 2 * RB_DEV + 1, dtype=jnp.int32)
    within = jax.random.randint(keys[1], (NRB, CAP), 0, RB_DEV, dtype=jnp.int32)
    opposite = jnp.mod(owner + row_count // 2, row_count) * RB_DEV + within
    picker = jax.random.randint(keys[2], (NRB, CAP), 0, 2, dtype=jnp.int32)
    columns = jnp.where(picker == 0, jnp.mod(row_ids + nearby, NRB), opposite)
    columns = columns.at[0, 0].set(0)
    columns = columns.at[NRB - 1, 0].set(NRB - 1)
    return columns.astype(jnp.int32)


def draw_counts(key, part):
    key = jax.random.fold_in(key, 23)
    keys = jax.random.split(key, 3)
    values = jax.random.randint(keys[0], (NRB,), 1, CAP + 1, dtype=jnp.int32)
    first_pos = jax.random.randint(keys[1], (), 0, NRB, dtype=jnp.int32)
    second_pos = jnp.mod(first_pos + 1 + jax.random.randint(keys[2], (), 0, max(NRB - 1, 1), dtype=jnp.int32), NRB)
    values = values.at[second_pos].set(1)
    values = values.at[first_pos].set(CAP)
    return values.astype(jnp.int32)


def block_scale(own_key, shape, pieces, smallest, top_value):
    def one(dim, shards_of):
        heights = jax.random.uniform(jax.random.fold_in(jax.random.fold_in(own_key, 6), dim), (shards_of,), jnp.float32, smallest / len(pieces), top_value / len(pieces))
        return jnp.repeat(jnp.exp(heights), shape[dim] // shards_of).reshape((-1,) + (1,) * (len(shape) - dim - 1))

    loudness = one(*pieces[0])
    for cut in pieces[1:]:
        loudness = loudness * one(*cut)
    return loudness


def scatter_about(own_key, extent, spread, reach, cuts=(), held_as=jnp.bfloat16):
    values = jax.random.normal(own_key, extent, jnp.float32) * spread
    if len(cuts) > 0:
        values = block_scale(own_key, extent, cuts, -0.22, 0.18) * values
    return jnp.clip(values, min=-reach, max=reach).astype(held_as)


def setup_inputs(seed: int = 0) -> dict:
    seeds = jax.random.split(jax.random.key(seed), 8)
    features = scatter_about(seeds[0], (NV, FIN), 1.0, 6.0, ((0, 64), (1, 4)))
    tiles = scatter_about(seeds[1], (NRB, CAP, TILE, TILE), (CAP * TILE // 2) ** -0.5, 0.1875, ((0, 64),))
    tile_cols = draw_tile_cols(jax.random.fold_in(seeds[7], 71), 0)
    counts = draw_counts(jax.random.fold_in(seeds[7], 71), 0)
    weight = scatter_about(seeds[4], (FIN, HID), FIN ** -0.5, 0.5, ((1, 4),))
    bias = scatter_about(seeds[5], (HID,), 0.5, 3.0, ((0, 4),), jnp.float32)
    cotangent = scatter_about(seeds[6], (NV, HID), 1.0, 6.0, ((0, 64), (1, 4)))
    return {"features": features, "tiles": tiles, "tile_cols": tile_cols, "counts": counts, "weight": weight, "bias": bias, "cotangent": cotangent}


def reference(features, tiles, tile_cols, counts, weight, bias, cotangent):
    block_count = tiles.shape[0]
    slot_count = tiles.shape[1]
    tile_size = tiles.shape[2]
    width_in = features.shape[1]
    blocks = features.reshape(block_count, tile_size, width_in)
    live = (jnp.arange(slot_count, dtype=jnp.int32)[None, :] < counts[:, None]).astype(jnp.float32)

    def aggregate(entry):
        tile_set, columns, alive = entry
        chosen = jnp.take(blocks, columns, axis=0).astype(jnp.float32) * alive[:, None, None]
        return jnp.einsum("crk,ckf->rf", tile_set.astype(jnp.float32), chosen)

    aggregated = lax.map(aggregate, (tiles, tile_cols, live))
    aggregated = aggregated.reshape(-1, width_in).astype(jnp.bfloat16)
    pre = jnp.dot(aggregated, weight, preferred_element_type=jnp.float32) + bias
    hidden = jax.nn.silu(pre).astype(jnp.bfloat16)
    sigma = jax.nn.sigmoid(pre)
    delta = (cotangent.astype(jnp.float32) * sigma * (1.0 + pre * (1.0 - sigma))).astype(jnp.bfloat16)
    grad_weight = jnp.dot(aggregated.T, delta, preferred_element_type=jnp.float32)
    grad_bias = jnp.sum(delta.astype(jnp.float32), axis=0)
    back_agg = jnp.dot(delta, weight.T, preferred_element_type=jnp.float32).astype(jnp.bfloat16)
    back_blocks = back_agg.reshape(block_count, tile_size, width_in)

    def scatter_step(total, entry):
        tile_set, columns, alive, back_block = entry
        contrib = jnp.einsum("crk,rf->ckf", tile_set.astype(jnp.float32), back_block.astype(jnp.float32))
        contrib = contrib * alive[:, None, None]
        return total.at[columns].add(contrib), None

    start_total = jnp.zeros((block_count, tile_size, width_in), jnp.float32)
    total, unused = lax.scan(scatter_step, start_total, (tiles, tile_cols, live, back_blocks))
    grad_features = total.reshape(-1, width_in).astype(jnp.bfloat16)
    return hidden, grad_weight, grad_bias, grad_features
```

```python
import functools

import jax
import jax.numpy as jnp
from jax import lax
from jax.experimental import pallas as pl
from jax.experimental.pallas import tpu as pltpu
from jax.sharding import PartitionSpec as P

F32 = jnp.float32
BF16 = jnp.bfloat16
TILE = 128
OFFSETS = (-2, -1, 0, 1, 2, None)
OWN = 2
NT = (((1,), (1,)), ((), ()))
NN = (((1,), (0,)), ((), ()))


def dot(a, b, dims):
    return lax.dot_general(a, b, dims, preferred_element_type=F32)


def kernel(
    n_row, n_rep, plane,
    cols_ref, counts_ref, bias_ref, ft_ref, tiles_ref, wt_ref, ct_ref,
    hid_out, gw_out, gb_out, gf_out,
    tiles, feats, cots, weights, biases, weight_fh, bias_col, keys_2d, table, table_s,
    agg_mine, agg, hid_mine, delta, back_mine, back, run, part, part_in,
    s1_mine, s1_in, s2_mine, s2_in, s3_mine, s3_in, gw_mine,
    sem_feat, sem_tile, sem_local,
    ss_feat, rs_feat, ss_pre, rs_pre, ss_agg, rs_agg, ss_back, rs_back, ss_hid, rs_hid,
    ss_s1, rs_s1, ss_s2, rs_s2, ss_s3, rs_s3, ss_s4, rs_s4, ss_part, rs_part,
):
    row = lax.axis_index("row")
    rep = lax.axis_index("rep")
    depth = n_row // plane
    layer = row // plane
    spot = row % plane
    n_blk = tiles_ref.shape[0]
    n_slot = tiles_ref.shape[1]
    per = n_blk // n_rep
    span = per * TILE
    none_feat = len(OFFSETS) * n_blk
    n_slots = n_blk * n_slot
    offsets = [n_row // 2 if o is None else o for o in OFFSETS]
    far_first = (5, 0, 4, 1, 3)
    order = tuple(range(1, n_rep)) + (0,)

    def block_at(p):
        return (per * rep + p) % n_blk

    def row_at(offset):
        return {"row": (row + offset + n_row) % n_row, "rep": rep}

    def rep_at(k):
        return {"row": row, "rep": (rep + k) % n_rep}

    def spot_at(k):
        return {"row": layer * plane + (spot + k) % plane, "rep": rep}

    def layer_at(k):
        return {"row": ((layer + k) % depth) * plane + spot, "rep": rep}

    def send(src, dst, ss, rs, where):
        return pltpu.make_async_remote_copy(
            src_ref=src, dst_ref=dst, send_sem=ss, recv_sem=rs,
            device_id=where, device_id_type=pl.DeviceIdType.MESH,
        )

    feat_loads = [
        pltpu.make_async_copy(ft_ref.at[:, TILE * b:TILE * (b + 1)], feats.at[OWN * n_blk + b], sem_feat.at[b])
        for b in range(n_blk)
    ]
    for c in feat_loads:
        c.start()
    mine = pl.ds(pl.multiple_of(rep * span, span), span)
    load_w = pltpu.make_async_copy(wt_ref, weights.at[rep], sem_local.at[0])
    load_c = pltpu.make_async_copy(ct_ref.at[:, mine], cots.at[rep], sem_local.at[1])
    load_w.start()
    load_c.start()
    tile_loads = []
    for k in range(n_rep):
        which = pl.ds(((rep + k) % n_rep) * per, per)
        tile_loads.append(
            pltpu.make_async_copy(tiles_ref.at[which], tiles.at[which], sem_tile.at[k])
        )
    for k in order:
        tile_loads[k].start()

    barrier = pltpu.get_barrier_semaphore()
    peers = [row_at(offsets[g]) for g in far_first]
    peers += [rep_at(k) for k in range(1, n_rep)]
    peers += [spot_at(k) for k in range(1, plane)]
    peers += [layer_at(k) for k in range(1, depth)]
    for where in peers:
        pl.semaphore_signal(barrier, inc=1, device_id=where, device_id_type=pl.DeviceIdType.MESH)
    biases[rep] = jnp.broadcast_to(jnp.pad(bias_ref[...], ((0, 0), (0, TILE - bias_ref.shape[1]))), (8, TILE))
    pl.semaphore_wait(barrier, len(peers))

    for c in feat_loads:
        c.wait()
    feat_sends = {
        g: send(
            feats.at[OWN * n_blk:(OWN + 1) * n_blk], feats.at[g * n_blk:(g + 1) * n_blk],
            ss_feat.at[g], rs_feat.at[g], row_at(-offsets[g]),
        )
        for g in far_first
    }
    for g in far_first:
        feat_sends[g].start()
    load_w.wait()
    pre_sends = []
    for k in range(1, n_rep):
        pre_sends.append(send(weights.at[rep], weights.at[rep], ss_pre.at[0, k - 1], rs_pre.at[0, k - 1], rep_at(k)))
        pre_sends.append(send(biases.at[rep], biases.at[rep], ss_pre.at[1, k - 1], rs_pre.at[1, k - 1], rep_at(k)))
        pre_sends.append(
            send(
                ct_ref.at[:, pl.ds(pl.multiple_of(((rep + k) % n_rep) * span, span), span)],
                cots.at[rep], ss_pre.at[2, k - 1], rs_pre.at[2, k - 1], rep_at(k),
            )
        )
    for c in pre_sends:
        c.start()

    cols = cols_ref[...]
    shape = cols.shape
    slot = lax.broadcasted_iota(jnp.int32, shape, 1)
    line = lax.broadcasted_iota(jnp.int32, shape, 0)
    count = jnp.zeros(shape, jnp.int32)
    for i in range(n_blk):
        count = jnp.where(line == i, counts_ref[i], count)
    group = jnp.minimum((cols // n_blk - row + 2 + n_row) % n_row, 5)
    key = jnp.where(slot < count, group * n_blk + cols % n_blk, none_feat)
    keys_2d[:, 0:n_slot] = key
    keys = jnp.concatenate([keys_2d[pl.ds(block_at(p), 1), 0:n_slot] for p in range(n_blk)], axis=1)
    by_lane = jnp.broadcast_to(keys, (n_slots, n_slots))
    by_line = by_lane.T
    up = lax.broadcasted_iota(jnp.int32, (n_slots, n_slots), 0)
    across = lax.broadcasted_iota(jnp.int32, (n_slots, n_slots), 1)
    before = jnp.max(jnp.where((by_line == by_lane) & (up < across), up, -1), axis=0, keepdims=True)
    last = jnp.max(jnp.where(by_line == across, up, -1), axis=0, keepdims=True)
    table[0:1, :] = keys
    table[1:2, :] = jnp.where(before < 0, n_slots, before)
    table[2:3, :] = jnp.where(last < 0, n_slots, last)
    table[3:8, :] = jnp.zeros((5, n_slots), jnp.int32)
    to_scalar = pltpu.make_async_copy(table, table_s, sem_local.at[2])
    to_scalar.start()
    feats[none_feat] = jnp.zeros(feats.shape[1:], BF16)
    run[n_slots] = jnp.zeros(run.shape[1:], F32)
    to_scalar.wait()

    for c in pre_sends:
        c.wait_recv()
    load_c.wait()
    n_hid = weights.shape[1]
    for j in range(n_rep):
        weight_fh[:, j * n_hid:(j + 1) * n_hid] = weights[j].astype(F32).T.astype(BF16)
        bias_col[j] = jnp.broadcast_to(biases[j, 0:1, :], (TILE, TILE)).T[0:n_hid, :]

    for g in far_first:
        feat_sends[g].wait_recv()

    agg_sends = []
    for k in order:
        tile_loads[k].wait()
        for q in range(per):
            p = k * per + q
            i = block_at(p)
            total = jnp.zeros((feats.shape[1], TILE), F32)
            for s in range(n_slot):
                total += dot(feats[table_s[0, p * n_slot + s]], tiles[i, s], NT)
            agg_mine[k, :, q * TILE:(q + 1) * TILE] = total.astype(BF16)
        if k:
            c = send(agg_mine.at[k], agg.at[rep], ss_agg.at[k - 1], rs_agg.at[k - 1], rep_at(k))
            c.start()
            agg_sends.append(c)
    agg[rep] = agg_mine[0]
    for c in agg_sends:
        c.wait_recv()

    whole = agg[...].reshape(n_rep * agg.shape[1], span)
    hid_sends = []
    for j in range(n_rep):
        wide_bias = jnp.concatenate([bias_col[j]] * (span // TILE), axis=1)
        pre = dot(weights[j], whole, NN) + wide_bias
        sigma = jax.nn.sigmoid(pre)
        hid_mine[j] = (pre * sigma).astype(BF16)
        delta[j] = (cots[j].astype(F32) * sigma * (1.0 + pre * (1.0 - sigma))).astype(BF16)
    deltas = delta[...].reshape(n_rep * n_hid, span)
    back_full = dot(weight_fh[...], deltas, NN).astype(BF16)
    back_mine[...] = back_full.reshape(back_mine.shape)
    back_sends = []
    for k in range(1, n_rep):
        c = send(back_mine.at[(rep + k) % n_rep], back.at[rep], ss_back.at[k - 1], rs_back.at[k - 1], rep_at(k))
        c.start()
        back_sends.append(c)
    back[rep] = back_mine[rep]
    for k in range(1, n_rep):
        c = send(hid_mine.at[(rep + k) % n_rep], hid_out.at[:, mine], ss_hid.at[k - 1], rs_hid.at[k - 1], rep_at(k))
        c.start()
        hid_sends.append(c)
    keep_hid = pltpu.make_async_copy(hid_mine.at[rep], hid_out.at[:, mine], sem_local.at[3])
    keep_hid.start()
    ones = jnp.ones((8, span), BF16)
    for j in range(n_rep):
        s1_mine[j, 0:n_hid, :] = dot(delta[j], whole, NT)
        s1_mine[j, n_hid:n_hid + 8, :] = jnp.pad(dot(ones, delta[j], NT), ((0, 0), (0, TILE - n_hid)))
    s1_sends = []
    for k in range(1, n_rep):
        c = send(s1_mine.at[(rep + k) % n_rep], s1_in.at[k - 1], ss_s1.at[k - 1], rs_s1.at[k - 1], rep_at(k))
        c.start()
        s1_sends.append(c)

    for c in back_sends:
        c.wait_recv()

    for k in range(n_rep):
        chunk = (rep + k) % n_rep
        for q in range(per):
            p = k * per + q
            i = block_at(p)
            lhs = back[chunk, :, q * TILE:(q + 1) * TILE]
            for s in range(n_slot):
                t = p * n_slot + s
                run[t] = dot(lhs, tiles[i, s], NN) + run[table_s[1, t]]

    part_sends = {}
    for g in far_first:
        for b in range(n_blk):
            part[g, b] = run[table_s[2, g * n_blk + b]].astype(BF16)
        c = send(part.at[g], part_in.at[g], ss_part.at[g], rs_part.at[g], row_at(offsets[g]))
        c.start()
        part_sends[g] = c

    for c in s1_sends:
        c.wait_recv()
    mid = s1_mine[rep]
    for k in range(1, n_rep):
        mid += s1_in[k - 1]
    for m in range(plane):
        s2_mine[m, 0:8, :] = mid[8 * m:8 * (m + 1), :]
        s2_mine[m, 8:16, :] = mid[n_hid:n_hid + 8, :]
    s2_sends = []
    for k in range(1, plane):
        c = send(s2_mine.at[(spot + k) % plane], s2_in.at[spot], ss_s2.at[k - 1], rs_s2.at[k - 1], spot_at(k))
        c.start()
        s2_sends.append(c)
    s2_in[spot] = s2_mine[spot]
    for c in s2_sends:
        c.wait_recv()
    s3_mine[...] = sum(s2_in[m] for m in range(plane))
    s3_sends = []
    for k in range(1, depth):
        c = send(s3_mine, s3_in.at[layer], ss_s3.at[k - 1], rs_s3.at[k - 1], layer_at(k))
        c.start()
        s3_sends.append(c)
    s3_in[layer] = s3_mine[...]
    for c in s3_sends:
        c.wait_recv()
    done = sum(s3_in[m] for m in range(depth))
    gw_mine[...] = done[0:8, :]
    gb_out[...] = done[8:16, :]
    my_rows = pl.ds(pl.multiple_of(spot * 8, 8), 8)
    s4_sends = []
    for k in range(1, plane):
        c = send(gw_mine, gw_out.at[my_rows, :], ss_s4.at[k - 1], rs_s4.at[k - 1], spot_at(k))
        c.start()
        s4_sends.append(c)
    keep_gw = pltpu.make_async_copy(gw_mine, gw_out.at[my_rows, :], sem_local.at[4])
    keep_gw.start()

    for g in far_first:
        part_sends[g].wait_recv()
    for b in range(n_blk):
        value = run[table_s[2, OWN * n_blk + b]]
        for g in far_first:
            value += part_in[g, b].astype(F32)
        gf_out[:, b * TILE:(b + 1) * TILE] = value.astype(BF16)

    for c in hid_sends + s4_sends:
        c.wait_recv()
    keep_hid.wait()
    keep_gw.wait()
    everything = [feat_sends[g] for g in far_first] + pre_sends + agg_sends + back_sends + hid_sends
    everything += s1_sends + s2_sends + s3_sends + s4_sends + [part_sends[g] for g in far_first]
    for c in everything:
        c.wait_send()


def body(n_row, n_rep, plane, features, tiles, tile_cols, counts, weight, bias, cotangent):
    n_blk, n_slot = tiles.shape[:2]
    rows, width = features.shape
    n_hid = weight.shape[1]
    fin = weight.shape[0]
    span = rows // n_rep
    depth = n_row // plane
    n_far = len(OFFSETS)
    n_slots = n_blk * n_slot
    dma = pltpu.SemaphoreType.DMA
    vmem = pl.BlockSpec(memory_space=pltpu.VMEM)
    smem = pl.BlockSpec(memory_space=pltpu.SMEM)
    hbm = pl.BlockSpec(memory_space=pl.ANY)

    def pair(*shape):
        return [dma(shape), dma(shape)]

    out = pl.pallas_call(
        functools.partial(kernel, n_row, n_rep, plane),
        out_shape=(
            jax.ShapeDtypeStruct((n_hid, rows), BF16),
            jax.ShapeDtypeStruct((n_hid, fin), F32),
            jax.ShapeDtypeStruct((8, TILE), F32),
            jax.ShapeDtypeStruct((width, rows), BF16),
        ),
        in_specs=[vmem, smem, vmem, hbm, hbm, hbm, hbm],
        out_specs=(vmem, vmem, vmem, vmem),
        scratch_shapes=[
            pltpu.VMEM(tiles.shape, BF16),
            pltpu.VMEM((len(OFFSETS) * n_blk + 1, width, TILE), BF16),
            pltpu.VMEM((n_rep, n_hid, span), BF16),
            pltpu.VMEM((n_rep, n_hid, fin), BF16),
            pltpu.VMEM((n_rep, 8, TILE), F32),
            pltpu.VMEM((fin, n_rep * n_hid), BF16),
            pltpu.VMEM((n_rep, n_hid, TILE), F32),
            pltpu.VMEM((n_blk, TILE), jnp.int32),
            pltpu.VMEM((8, TILE), jnp.int32),
            pltpu.SMEM((8, TILE), jnp.int32),
            pltpu.VMEM((n_rep, width, span), BF16),
            pltpu.VMEM((n_rep, width, span), BF16),
            pltpu.VMEM((n_rep, n_hid, span), BF16),
            pltpu.VMEM((n_rep, n_hid, span), BF16),
            pltpu.VMEM((n_rep, width, span), BF16),
            pltpu.VMEM((n_rep, width, span), BF16),
            pltpu.VMEM((n_slots + 1, width, TILE), F32),
            pltpu.VMEM((n_far, n_blk, width, TILE), BF16),
            pltpu.VMEM((n_far, n_blk, width, TILE), BF16),
            pltpu.VMEM((n_rep, n_hid + 8, TILE), F32),
            pltpu.VMEM((n_rep - 1, n_hid + 8, TILE), F32),
            pltpu.VMEM((plane, 16, TILE), F32),
            pltpu.VMEM((plane, 16, TILE), F32),
            pltpu.VMEM((16, TILE), F32),
            pltpu.VMEM((depth, 16, TILE), F32),
            pltpu.VMEM((8, TILE), F32),
            dma((n_blk,)),
            dma((n_rep,)),
            dma((5,)),
            *pair(n_far),
            *pair(3, n_rep - 1),
            *pair(n_rep - 1),
            *pair(n_rep - 1),
            *pair(n_rep - 1),
            *pair(n_rep - 1),
            *pair(plane - 1),
            *pair(depth - 1),
            *pair(plane - 1),
            *pair(n_far),
        ],
        compiler_params=pltpu.CompilerParams(
            collective_id=0, has_side_effects=True, vmem_limit_bytes=32 * 1024 * 1024
        ),
        cost_estimate=pl.CostEstimate(
            flops=4 * n_slots * TILE * TILE * width, bytes_accessed=tiles.size * 2, transcendentals=span * n_rep * n_hid
        ),
    )(
        tile_cols, counts, bias.reshape(1, n_hid), features.T, tiles, weight.T, cotangent.T,
    )
    hidden, grad_weight, grad_bias, grad_features = out
    return hidden.T, grad_weight.T, grad_bias[0, :n_hid], grad_features.T


def solution(mesh):
    in_specs = (
        P("row", "rep"),
        P("row", None, None, None),
        P("row", None),
        P("row"),
        P(None, "rep"),
        P("rep"),
        P("row", "rep"),
    )
    out_specs = (P("row", "rep"), P(None, "rep"), P("rep"), P("row", "rep"))
    n_row, n_rep = mesh.shape["row"], mesh.shape["rep"]
    step = functools.partial(body, n_row, n_rep, 8)
    return jax.shard_map(step, mesh=mesh, in_specs=in_specs, out_specs=out_specs, check_vma=False)
```

```python
import functools

import jax
import jax.numpy as jnp
from jax import lax
from jax.experimental import pallas as pl
from jax.experimental.pallas import tpu as pltpu
from jax.sharding import PartitionSpec as P

F32 = jnp.float32
BF16 = jnp.bfloat16
TILE = 128
OFFSETS = (-2, -1, 0, 1, 2, None)
OWN = 2
NT = (((1,), (1,)), ((), ()))
NN = (((1,), (0,)), ((), ()))


def dot(a, b, dims):
    return lax.dot_general(a, b, dims, preferred_element_type=F32)


def kernel(
    n_row, n_rep, plane,
    cols_hbm, counts_hbm, bias_hbm, ft_ref, tiles_ref, wt_ref, ct_ref,
    hid_out, gw_out, gb_out, gf_out,
    cols_ref, counts_ref, bias_ref, tiles, feats, cots, weights, biases, weight_fh, bias_col, keys_2d, table, table_s,
    agg_mine, agg, hid_mine, delta, back_mine, back, run, part, part_in,
    team_mine, team_in, s3_mine, s3_in, gw_mine, gb_mine, gf_mine,
    sem_feat, sem_tile, sem_local,
    ss_feat, rs_feat, ss_pre, rs_pre, ss_agg, rs_agg, ss_back, rs_back, ss_hid, rs_hid,
    ss_team, rs_team, ss_s3, rs_s3, ss_s4, rs_s4, ss_part, rs_part,
):
    row = lax.axis_index("row")
    rep = lax.axis_index("rep")
    depth = n_row // plane
    layer = row // plane
    spot = row % plane
    n_blk = tiles_ref.shape[0]
    n_slot = tiles_ref.shape[1]
    per = n_blk // n_rep
    span = per * TILE
    none_feat = len(OFFSETS) * n_blk
    n_slots = n_blk * n_slot
    offsets = [n_row // 2 if o is None else o for o in OFFSETS]
    far_first = (5, 0, 4, 1, 3)
    hops = [min(k, n_rep - k) for k in range(n_rep)]
    near_last = sorted(range(1, n_rep), key=lambda k: -hops[k])
    order = near_last + [0]
    team = [(k, m) for k in range(n_rep) for m in range(plane) if (k, m) != (0, 0)]
    back_order = [0] + near_last[::-1]

    def block_at(p, q=0):
        return ((rep + back_order[p // per]) % n_rep) * per + p % per + q

    def row_at(offset):
        return {"row": (row + offset + n_row) % n_row, "rep": rep}

    def rep_at(k):
        return {"row": row, "rep": (rep + k) % n_rep}

    def team_at(k, m):
        return {"row": layer * plane + (spot + m) % plane, "rep": (rep + k) % n_rep}

    def spot_at(k):
        return {"row": layer * plane + (spot + k) % plane, "rep": rep}

    def layer_at(k):
        return {"row": ((layer + k) % depth) * plane + spot, "rep": rep}

    def send(src, dst, ss, rs, where):
        return pltpu.make_async_remote_copy(
            src_ref=src, dst_ref=dst, send_sem=ss, recv_sem=rs,
            device_id=where, device_id_type=pl.DeviceIdType.MESH,
        )

    barrier = pltpu.get_barrier_semaphore()
    peers = [row_at(offsets[g]) for g in far_first]
    peers += [team_at(*o) for o in team]
    peers += [layer_at(k) for k in range(1, depth)]
    for where in peers:
        pl.semaphore_signal(barrier, inc=1, device_id=where, device_id_type=pl.DeviceIdType.MESH)

    feat_loads = [
        pltpu.make_async_copy(ft_ref.at[:, TILE * b:TILE * (b + 1)], feats.at[OWN * n_blk + b], sem_feat.at[b])
        for b in range(n_blk)
    ]
    for c in feat_loads:
        c.start()
    mine = pl.ds(pl.multiple_of(rep * span, span), span)
    load_w = pltpu.make_async_copy(wt_ref, weights.at[rep], sem_local.at[0])
    load_c = pltpu.make_async_copy(ct_ref.at[:, mine], cots.at[rep], sem_local.at[1])
    load_cols = pltpu.make_async_copy(cols_hbm, cols_ref, sem_local.at[5])
    load_counts = pltpu.make_async_copy(counts_hbm, counts_ref, sem_local.at[6])
    load_bias = pltpu.make_async_copy(bias_hbm, bias_ref, sem_local.at[7])
    for c in (load_w, load_bias, load_cols, load_counts, load_c):
        c.start()
    tile_loads = []
    for k in range(n_rep):
        which = pl.ds(((rep + k) % n_rep) * per, per)
        tile_loads.append(
            pltpu.make_async_copy(tiles_ref.at[which], tiles.at[which], sem_tile.at[k])
        )
    for k in order:
        tile_loads[k].start()

    pl.semaphore_wait(barrier, len(peers))

    for c in feat_loads:
        c.wait()
    feat_sends = {
        g: send(
            feats.at[OWN * n_blk:(OWN + 1) * n_blk], feats.at[g * n_blk:(g + 1) * n_blk],
            ss_feat.at[g], rs_feat.at[g], row_at(-offsets[g]),
        )
        for g in far_first
    }
    for g in far_first:
        feat_sends[g].start()
    load_w.wait()
    load_bias.wait()
    biases[rep] = jnp.broadcast_to(jnp.pad(bias_ref[...], ((0, 0), (0, TILE - bias_ref.shape[1]))), (8, TILE))
    pre_sends = []
    for k in range(1, n_rep):
        pre_sends.append(send(weights.at[rep], weights.at[rep], ss_pre.at[0, k - 1], rs_pre.at[0, k - 1], rep_at(k)))
        pre_sends.append(send(biases.at[rep], biases.at[rep], ss_pre.at[1, k - 1], rs_pre.at[1, k - 1], rep_at(k)))
        pre_sends.append(
            send(
                ct_ref.at[:, pl.ds(pl.multiple_of(((rep + k) % n_rep) * span, span), span)],
                cots.at[rep], ss_pre.at[2, k - 1], rs_pre.at[2, k - 1], rep_at(k),
            )
        )
    for c in pre_sends:
        c.start()

    load_cols.wait()
    load_counts.wait()
    cols = cols_ref[...]
    shape = cols.shape
    slot = lax.broadcasted_iota(jnp.int32, shape, 1)
    line = lax.broadcasted_iota(jnp.int32, shape, 0)
    count = jnp.zeros(shape, jnp.int32)
    for i in range(n_blk):
        count = jnp.where(line == i, counts_ref[i], count)
    group = jnp.minimum((cols // n_blk - row + 2 + n_row) % n_row, 5)
    key = jnp.where(slot < count, group * n_blk + cols % n_blk, none_feat)
    keys_2d[:, 0:n_slot] = key
    keys = jnp.concatenate([keys_2d[pl.ds(block_at(p), 1), 0:n_slot] for p in range(n_blk)], axis=1)
    by_lane = jnp.broadcast_to(keys, (n_slots, n_slots))
    by_line = by_lane.T
    up = lax.broadcasted_iota(jnp.int32, (n_slots, n_slots), 0)
    across = lax.broadcasted_iota(jnp.int32, (n_slots, n_slots), 1)
    before = jnp.max(jnp.where((by_line == by_lane) & (up < across), up, -1), axis=0, keepdims=True)
    last = jnp.max(jnp.where(by_line == across, up, -1), axis=0, keepdims=True)
    table[0:1, :] = keys
    table[1:2, :] = jnp.where(before < 0, n_slots, before)
    table[2:3, :] = jnp.where(last < 0, n_slots, last)
    table[3:8, :] = jnp.zeros((5, n_slots), jnp.int32)
    to_scalar = pltpu.make_async_copy(table, table_s, sem_local.at[2])
    to_scalar.start()
    feats[none_feat] = jnp.zeros(feats.shape[1:], BF16)
    run[n_slots] = jnp.zeros(run.shape[1:], F32)
    to_scalar.wait()

    for c in pre_sends:
        c.wait_recv()
    load_c.wait()
    n_hid = weights.shape[1]
    for j in range(n_rep):
        weight_fh[:, j * n_hid:(j + 1) * n_hid] = weights[j].astype(F32).T.astype(BF16)
        bias_col[j] = jnp.broadcast_to(biases[j, 0:1, :], (TILE, TILE)).T[0:n_hid, :]

    for g in far_first:
        feat_sends[g].wait_recv()

    agg_sends = []
    for k in order:
        tile_loads[k].wait()

        @pl.loop(0, per)
        def _(q, k=k):
            p = back_order.index(k) * per + q
            i = ((rep + k) % n_rep) * per + q
            total = jnp.zeros((feats.shape[1], TILE), F32)
            for s in range(n_slot):
                total += dot(feats[table_s[0, p * n_slot + s]], tiles[i, s], NT)
            agg_mine[k, q] = total.astype(BF16)

        if k:
            c = send(agg_mine.at[k], agg.at[rep], ss_agg.at[k - 1], rs_agg.at[k - 1], rep_at(k))
            c.start()
            agg_sends.append(c)
    agg[rep] = agg_mine[0]
    for c in agg_sends:
        c.wait_recv()

    width = agg.shape[2]
    whole = jnp.concatenate([agg[:, q].reshape(n_rep * width, TILE) for q in range(per)], axis=1)
    hid_sends = []
    for j in range(n_rep):
        wide_bias = jnp.concatenate([bias_col[j]] * (span // TILE), axis=1)
        pre = dot(weights[j], whole, NN) + wide_bias
        sigma = jax.nn.sigmoid(pre)
        hid_mine[j] = (pre * sigma).astype(BF16)
        delta[j] = (cots[j].astype(F32) * sigma * (1.0 + pre * (1.0 - sigma))).astype(BF16)
    deltas = delta[...].reshape(n_rep * n_hid, span)
    back_full = dot(weight_fh[...], deltas, NN).astype(BF16)
    for q in range(per):
        back_mine[:, q] = back_full[:, q * TILE:(q + 1) * TILE].reshape(n_rep, width, TILE)
    back_sends = []
    for k in range(1, n_rep):
        c = send(back_mine.at[(rep + k) % n_rep], back.at[rep], ss_back.at[k - 1], rs_back.at[k - 1], rep_at(k))
        c.start()
        back_sends.append(c)
    back[rep] = back_mine[rep]
    ones = jnp.ones((8, span), BF16)
    team_sends = []
    for j in range(n_rep):
        grad = dot(delta[j], whole, NT)
        bias_grad = jnp.pad(dot(ones, delta[j], NT), ((0, 0), (0, TILE - n_hid)))
        for m in range(plane):
            team_mine[j, m, 0:8, :] = grad[8 * m:8 * (m + 1), :]
            team_mine[j, m, 8:16, :] = bias_grad
    for n, (k, m) in enumerate(team):
        c = send(
            team_mine.at[(rep + k) % n_rep, (spot + m) % plane], team_in.at[rep, spot],
            ss_team.at[n], rs_team.at[n], team_at(k, m),
        )
        c.start()
        team_sends.append(c)
    team_in[rep, spot] = team_mine[rep, spot]
    for k in range(1, n_rep):
        c = send(hid_mine.at[(rep + k) % n_rep], hid_out.at[:, mine], ss_hid.at[k - 1], rs_hid.at[k - 1], rep_at(k))
        c.start()
        hid_sends.append(c)
    keep_hid = pltpu.make_async_copy(hid_mine.at[rep], hid_out.at[:, mine], sem_local.at[3])
    keep_hid.start()

    for n, k in enumerate(back_order):
        if k:
            back_sends[n_rep - k - 1].wait_recv()

        @pl.loop(0, per)
        def _(q, n=n, k=k):
            chunk = (rep + k) % n_rep
            lhs = back[chunk, q]
            for s in range(n_slot):
                t = (n * per + q) * n_slot + s
                run[t] = dot(lhs, tiles[chunk * per + q, s], NN) + run[table_s[1, t]]

    part_sends = {}
    for g in far_first:
        for b in range(n_blk):
            part[g, b] = run[table_s[2, g * n_blk + b]].astype(BF16)
        c = send(part.at[g], part_in.at[g], ss_part.at[g], rs_part.at[g], row_at(offsets[g]))
        c.start()
        part_sends[g] = c

    for c in team_sends:
        c.wait_recv()
    s3_mine[...] = sum(team_in[k, m] for k in range(n_rep) for m in range(plane))
    s3_sends = []
    for k in range(1, depth):
        c = send(s3_mine, s3_in.at[layer], ss_s3.at[k - 1], rs_s3.at[k - 1], layer_at(k))
        c.start()
        s3_sends.append(c)
    s3_in[layer] = s3_mine[...]
    for g in far_first:
        part_sends[g].wait_recv()
    for b in range(n_blk):
        value = run[table_s[2, OWN * n_blk + b]]
        for g in far_first:
            value += part_in[g, b].astype(F32)
        gf_mine[:, b * TILE:(b + 1) * TILE] = value.astype(BF16)
    keep_gf = pltpu.make_async_copy(gf_mine, gf_out, sem_local.at[2])
    keep_gf.start()

    for c in s3_sends:
        c.wait_recv()
    done = sum(s3_in[m] for m in range(depth))
    gw_mine[...] = done[0:8, :]
    gb_mine[...] = done[8:16, :]
    keep_gb = pltpu.make_async_copy(gb_mine, gb_out, sem_local.at[5])
    keep_gb.start()
    my_rows = pl.ds(pl.multiple_of(spot * 8, 8), 8)
    s4_sends = []
    for k in range(1, plane):
        c = send(gw_mine, gw_out.at[my_rows, :], ss_s4.at[k - 1], rs_s4.at[k - 1], spot_at(k))
        c.start()
        s4_sends.append(c)
    keep_gw = pltpu.make_async_copy(gw_mine, gw_out.at[my_rows, :], sem_local.at[4])
    keep_gw.start()

    for c in hid_sends + s4_sends:
        c.wait_recv()
    keep_hid.wait()
    keep_gw.wait()
    keep_gb.wait()
    keep_gf.wait()
    everything = [feat_sends[g] for g in far_first] + pre_sends + agg_sends + back_sends + hid_sends
    everything += team_sends + s3_sends + s4_sends + [part_sends[g] for g in far_first]
    for c in everything:
        c.wait_send()


def finish(hid_in, gw_in, gb_in, gf_in, hid_out, gw_out, gb_out, gf_out, gb, sems):
    pairs = ((hid_in, hid_out), (gf_in, gf_out), (gw_in, gw_out), (gb_in, gb))
    copies = [pltpu.make_async_copy(a, b, sems.at[n]) for n, (a, b) in enumerate(pairs)]
    for c in copies:
        c.start()
    copies[3].wait()
    gb_out[...] = gb[0:1, 0:gb_out.shape[1]]
    for c in copies[:3]:
        c.wait()


def body(n_row, n_rep, plane, features, tiles, tile_cols, counts, weight, bias, cotangent):
    n_blk, n_slot = tiles.shape[:2]
    rows, width = features.shape
    n_hid = weight.shape[1]
    fin = weight.shape[0]
    span = rows // n_rep
    depth = n_row // plane
    n_far = len(OFFSETS)
    n_slots = n_blk * n_slot
    dma = pltpu.SemaphoreType.DMA
    vmem = pl.BlockSpec(memory_space=pltpu.VMEM)
    smem = pl.BlockSpec(memory_space=pltpu.SMEM)
    hbm = pl.BlockSpec(memory_space=pltpu.HBM)

    def pair(*shape):
        return [dma(shape), dma(shape)]

    out = pl.pallas_call(
        functools.partial(kernel, n_row, n_rep, plane),
        out_shape=(
            jax.ShapeDtypeStruct((n_hid, rows), BF16),
            jax.ShapeDtypeStruct((n_hid, fin), F32),
            jax.ShapeDtypeStruct((8, TILE), F32),
            jax.ShapeDtypeStruct((width, rows), BF16),
        ),
        in_specs=[hbm] * 7,
        out_specs=(hbm, hbm, hbm, hbm),
        scratch_shapes=[
            pltpu.VMEM(tile_cols.shape, jnp.int32),
            pltpu.SMEM(counts.shape, jnp.int32),
            pltpu.VMEM((1, n_hid), F32),
            pltpu.VMEM(tiles.shape, BF16),
            pltpu.VMEM((len(OFFSETS) * n_blk + 1, width, TILE), BF16),
            pltpu.VMEM((n_rep, n_hid, span), BF16),
            pltpu.VMEM((n_rep, n_hid, fin), BF16),
            pltpu.VMEM((n_rep, 8, TILE), F32),
            pltpu.VMEM((fin, n_rep * n_hid), BF16),
            pltpu.VMEM((n_rep, n_hid, TILE), F32),
            pltpu.VMEM((n_blk, TILE), jnp.int32),
            pltpu.VMEM((8, TILE), jnp.int32),
            pltpu.SMEM((8, TILE), jnp.int32),
            pltpu.VMEM((n_rep, n_blk // n_rep, width, TILE), BF16),
            pltpu.VMEM((n_rep, n_blk // n_rep, width, TILE), BF16),
            pltpu.VMEM((n_rep, n_hid, span), BF16),
            pltpu.VMEM((n_rep, n_hid, span), BF16),
            pltpu.VMEM((n_rep, n_blk // n_rep, width, TILE), BF16),
            pltpu.VMEM((n_rep, n_blk // n_rep, width, TILE), BF16),
            pltpu.VMEM((n_slots + 1, width, TILE), F32),
            pltpu.VMEM((n_far, n_blk, width, TILE), BF16),
            pltpu.VMEM((n_far, n_blk, width, TILE), BF16),
            pltpu.VMEM((n_rep, plane, 16, TILE), F32),
            pltpu.VMEM((n_rep, plane, 16, TILE), F32),
            pltpu.VMEM((16, TILE), F32),
            pltpu.VMEM((depth, 16, TILE), F32),
            pltpu.VMEM((8, TILE), F32),
            pltpu.VMEM((8, TILE), F32),
            pltpu.VMEM((width, rows), BF16),
            dma((n_blk,)),
            dma((n_rep,)),
            dma((8,)),
            *pair(n_far),
            *pair(3, n_rep - 1),
            *pair(n_rep - 1),
            *pair(n_rep - 1),
            *pair(n_rep - 1),
            *pair(n_rep * plane - 1),
            *pair(depth - 1),
            *pair(plane - 1),
            *pair(n_far),
        ],
        compiler_params=pltpu.CompilerParams(
            collective_id=0, has_side_effects=True, vmem_limit_bytes=62 * 1024 * 1024
        ),
        cost_estimate=pl.CostEstimate(
            flops=4 * n_slots * TILE * TILE * width, bytes_accessed=tiles.size * 2, transcendentals=span * n_rep * n_hid
        ),
    )(
        tile_cols, counts, bias.reshape(1, n_hid), features.T, tiles, weight.T, cotangent.T,
    )
    hidden, grad_weight, grad_bias, grad_features = pl.pallas_call(
        finish,
        out_shape=(
            jax.ShapeDtypeStruct((n_hid, rows), BF16),
            jax.ShapeDtypeStruct((n_hid, fin), F32),
            jax.ShapeDtypeStruct((1, n_hid), F32),
            jax.ShapeDtypeStruct((width, rows), BF16),
        ),
        in_specs=[hbm] * 4,
        out_specs=(hbm, hbm, vmem, hbm),
        scratch_shapes=[pltpu.VMEM((8, TILE), F32), dma((4,))],
        compiler_params=pltpu.CompilerParams(vmem_limit_bytes=62 * 1024 * 1024),
    )(*out)
    return hidden.T, grad_weight.T, grad_bias.reshape(n_hid), grad_features.T


def solution(mesh):
    in_specs = (
        P("row", "rep"),
        P("row", None, None, None),
        P("row", None),
        P("row"),
        P(None, "rep"),
        P("rep"),
        P("row", "rep"),
    )
    out_specs = (P("row", "rep"), P(None, "rep"), P("rep"), P("row", "rep"))
    n_row, n_rep = mesh.shape["row"], mesh.shape["rep"]
    step = functools.partial(body, n_row, n_rep, 8)
    return jax.shard_map(step, mesh=mesh, in_specs=in_specs, out_specs=out_specs, check_vma=False)
```

```python
import functools

import jax
import jax.numpy as jnp
from jax import lax
from jax.experimental import pallas as pl
from jax.experimental.pallas import tpu as pltpu
from jax.sharding import PartitionSpec as P

F32 = jnp.float32
BF16 = jnp.bfloat16
TILE = 128
OFFSETS = (-2, -1, 0, 1, 2, None)
OWN = 2
FAR = 5
GROUP = 2
BACK_GROUP = 2
NT = (((1,), (1,)), ((), ()))
NN = (((1,), (0,)), ((), ()))


def dot(a, b, dims):
    return lax.dot_general(a, b, dims, preferred_element_type=F32)


def join(parts):
    return jnp.concatenate(parts, axis=1) if len(parts) > 1 else parts[0]


def kernel(
    n_row, n_rep, plane,
    cols_hbm, counts_hbm, bias_hbm, ft_ref, tiles_ref, wt_ref, ct_ref,
    hid_out, gw_out, gb_out, gf_out,
    cols_ref, counts_ref, bias_ref, tiles, feats, cots, weights, biases, weight_fh, bias_col, keys_2d, table, table_s,
    agg_mine, agg, hid_mine, delta, back_mine, back, run, part, part_in,
    team_mine, team_in, s3_mine, s3_in, gw_mine, gb_mine, gf_mine,
    sem_feat, sem_tile, sem_local,
    ss_feat, rs_feat, ss_pre, rs_pre, ss_agg, rs_agg, ss_back, rs_back, ss_hid, rs_hid,
    ss_team, rs_team, ss_s3, rs_s3, ss_s4, rs_s4, ss_part, rs_part,
):
    row = lax.axis_index("row")
    rep = lax.axis_index("rep")
    depth = n_row // plane
    layer = row // plane
    spot = row % plane
    n_blk = tiles_ref.shape[0]
    n_slot = tiles_ref.shape[1]
    per = n_blk // n_rep
    span = per * TILE
    none_feat = len(OFFSETS) * n_blk
    n_slots = n_blk * n_slot
    offsets = [n_row // 2 if o is None else o for o in OFFSETS]
    far_first = (5, 0, 4, 1, 3)
    hops = [min(k, n_rep - k) for k in range(n_rep)]
    near_last = sorted(range(1, n_rep), key=lambda k: -hops[k])
    order = near_last + [0]
    team = [(k, m) for k in range(n_rep) for m in range(plane) if (k, m) != (0, 0)]
    team.sort(key=lambda o: -hops[o[0]] - min(o[1], plane - o[1]) / 2)
    spots = sorted(range(1, plane), key=lambda m: -min(m, plane - m))
    layers = sorted(range(1, depth), key=lambda m: -min(m, depth - m))
    back_order = [0] + near_last[::-1]

    def block_at(p, q=0):
        return ((rep + back_order[p // per]) % n_rep) * per + p % per + q

    def row_at(offset):
        return {"row": (row + offset + n_row) % n_row, "rep": rep}

    def rep_at(k):
        return {"row": row, "rep": (rep + k) % n_rep}

    def team_at(k, m):
        return {"row": layer * plane + (spot + m) % plane, "rep": (rep + k) % n_rep}

    def spot_at(k):
        return {"row": layer * plane + (spot + k) % plane, "rep": rep}

    def layer_at(k):
        return {"row": ((layer + k) % depth) * plane + spot, "rep": rep}

    def send(src, dst, ss, rs, where):
        return pltpu.make_async_remote_copy(
            src_ref=src, dst_ref=dst, send_sem=ss, recv_sem=rs,
            device_id=where, device_id_type=pl.DeviceIdType.MESH,
        )

    barrier = pltpu.get_barrier_semaphore()
    peers = [row_at(offsets[g]) for g in far_first]
    peers += [team_at(*o) for o in team]
    peers += [layer_at(k) for k in layers]
    for where in peers:
        pl.semaphore_signal(barrier, inc=1, device_id=where, device_id_type=pl.DeviceIdType.MESH)

    feat_loads = [
        pltpu.make_async_copy(ft_ref.at[:, TILE * b:TILE * (b + 1)], feats.at[OWN * n_blk + b], sem_feat.at[b])
        for b in range(n_blk)
    ]
    for c in feat_loads:
        c.start()
    mine = pl.ds(pl.multiple_of(rep * span, span), span)
    load_w = pltpu.make_async_copy(wt_ref, weights.at[rep], sem_local.at[0])
    load_c = pltpu.make_async_copy(ct_ref.at[:, mine], cots.at[rep], sem_local.at[1])
    load_cols = pltpu.make_async_copy(cols_hbm, cols_ref, sem_local.at[5])
    load_counts = pltpu.make_async_copy(counts_hbm, counts_ref, sem_local.at[6])
    load_bias = pltpu.make_async_copy(bias_hbm, bias_ref, sem_local.at[7])
    for c in (load_w, load_bias, load_cols, load_counts, load_c):
        c.start()
    tile_loads = []
    for k in range(n_rep):
        which = pl.ds(((rep + k) % n_rep) * per, per)
        tile_loads.append(
            pltpu.make_async_copy(tiles_ref.at[which], tiles.at[which], sem_tile.at[k])
        )
    for k in order:
        tile_loads[k].start()

    pl.semaphore_wait(barrier, len(peers))

    for c in feat_loads:
        c.wait()
    feat_sends = {
        g: send(
            feats.at[OWN * n_blk:(OWN + 1) * n_blk], feats.at[g * n_blk:(g + 1) * n_blk],
            ss_feat.at[g], rs_feat.at[g], row_at(-offsets[g]),
        )
        for g in far_first
    }
    for g in far_first:
        feat_sends[g].start()
    load_w.wait()
    load_bias.wait()
    biases[rep] = jnp.broadcast_to(jnp.pad(bias_ref[...], ((0, 0), (0, TILE - bias_ref.shape[1]))), (8, TILE))
    pre_sends = []
    for k in range(1, n_rep):
        pre_sends.append(send(weights.at[rep], weights.at[rep], ss_pre.at[0, k - 1], rs_pre.at[0, k - 1], rep_at(k)))
        pre_sends.append(send(biases.at[rep], biases.at[rep], ss_pre.at[1, k - 1], rs_pre.at[1, k - 1], rep_at(k)))
        pre_sends.append(
            send(
                ct_ref.at[:, pl.ds(pl.multiple_of(((rep + k) % n_rep) * span, span), span)],
                cots.at[rep], ss_pre.at[2, k - 1], rs_pre.at[2, k - 1], rep_at(k),
            )
        )
    for c in pre_sends:
        c.start()

    load_cols.wait()
    load_counts.wait()
    cols = cols_ref[...]
    shape = cols.shape
    slot = lax.broadcasted_iota(jnp.int32, shape, 1)
    line = lax.broadcasted_iota(jnp.int32, shape, 0)
    count = jnp.zeros(shape, jnp.int32)
    for i in range(n_blk):
        count = jnp.where(line == i, counts_ref[i], count)
    group = jnp.minimum((cols // n_blk - row + 2 + n_row) % n_row, 5)
    key = jnp.where(slot < count, group * n_blk + cols % n_blk, none_feat)
    keys_2d[:, 0:n_slot] = key
    keys = jnp.concatenate([keys_2d[pl.ds(block_at(p), 1), 0:n_slot] for p in range(n_blk)], axis=1)
    by_lane = jnp.broadcast_to(keys, (n_slots, n_slots))
    by_line = by_lane.T
    up = lax.broadcasted_iota(jnp.int32, (n_slots, n_slots), 0)
    across = lax.broadcasted_iota(jnp.int32, (n_slots, n_slots), 1)
    before = jnp.max(jnp.where((by_line == by_lane) & (up < across), up, -1), axis=0, keepdims=True)
    last = jnp.max(jnp.where(by_line == across, up, -1), axis=0, keepdims=True)
    table[0:1, :] = keys
    table[1:2, :] = jnp.where(before < 0, n_slots, before)
    table[2:3, :] = jnp.where(last < 0, n_slots, last)
    table[3:8, :] = jnp.zeros((5, n_slots), jnp.int32)
    to_scalar = pltpu.make_async_copy(table, table_s, sem_local.at[2])
    to_scalar.start()
    feats[none_feat] = jnp.zeros(feats.shape[1:], BF16)
    run[n_slots] = jnp.zeros(run.shape[1:], F32)
    to_scalar.wait()

    for c in pre_sends:
        c.wait_recv()
    load_c.wait()
    n_hid = weights.shape[1]
    for j in range(n_rep):
        weight_fh[:, j * n_hid:(j + 1) * n_hid] = weights[j].astype(F32).T.astype(BF16)
        bias_col[j] = jnp.broadcast_to(biases[j, 0:1, :], (TILE, TILE)).T[0:n_hid, :]

    for g in far_first:
        feat_sends[g].wait_recv()

    agg_sends = []
    for k in order:
        tile_loads[k].wait()

        @pl.loop(0, per)
        def _(q, k=k):
            p = back_order.index(k) * per + q
            i = ((rep + k) % n_rep) * per + q
            total = jnp.zeros((feats.shape[1], TILE), F32)
            for s in range(0, n_slot, GROUP):
                some = [feats[table_s[0, p * n_slot + s + t]] for t in range(GROUP)]
                total += dot(join(some), join([tiles[i, s + t] for t in range(GROUP)]), NT)
            agg_mine[k, q] = total.astype(BF16)

        if k:
            c = send(agg_mine.at[k], agg.at[rep], ss_agg.at[k - 1], rs_agg.at[k - 1], rep_at(k))
            c.start()
            agg_sends.append(c)
    agg[rep] = agg_mine[0]
    for c in agg_sends:
        c.wait_recv()

    width = agg.shape[2]
    whole = jnp.concatenate([agg[:, q].reshape(n_rep * width, TILE) for q in range(per)], axis=1)
    hid_sends = []
    for j in range(n_rep):
        wide_bias = jnp.concatenate([bias_col[j]] * (span // TILE), axis=1)
        pre = dot(weights[j], whole, NN) + wide_bias
        sigma = jax.nn.sigmoid(pre)
        hid_mine[j] = (pre * sigma).astype(BF16)
        delta[j] = (cots[j].astype(F32) * sigma * (1.0 + pre * (1.0 - sigma))).astype(BF16)
    deltas = delta[...].reshape(n_rep * n_hid, span)
    back_full = dot(weight_fh[...], deltas, NN).astype(BF16)
    for q in range(per):
        back_mine[:, q] = back_full[:, q * TILE:(q + 1) * TILE].reshape(n_rep, width, TILE)
    back_sends = []
    for k in range(1, n_rep):
        c = send(back_mine.at[(rep + k) % n_rep], back.at[rep], ss_back.at[k - 1], rs_back.at[k - 1], rep_at(k))
        c.start()
        back_sends.append(c)
    back[rep] = back_mine[rep]
    ones = jnp.ones((8, span), BF16)
    team_sends = []
    for j in range(n_rep):
        grad = dot(delta[j], whole, NT)
        bias_grad = jnp.pad(dot(ones, delta[j], NT)[0:1, :], ((0, 0), (0, TILE - n_hid)))
        for m in range(plane):
            team_mine[j, m, 0:8, :] = grad[8 * m:8 * (m + 1), :]
            team_mine[j, m, 8:9, :] = bias_grad
    for n, (k, m) in enumerate(team):
        c = send(
            team_mine.at[(rep + k) % n_rep, (spot + m) % plane, 0:9], team_in.at[rep, spot, 0:9],
            ss_team.at[n], rs_team.at[n], team_at(k, m),
        )
        c.start()
        team_sends.append(c)
    team_in[rep, spot, 0:9] = team_mine[rep, spot, 0:9]
    for k in range(1, n_rep):
        c = send(hid_mine.at[(rep + k) % n_rep], hid_out.at[:, mine], ss_hid.at[k - 1], rs_hid.at[k - 1], rep_at(k))
        c.start()
        hid_sends.append(c)
    keep_hid = pltpu.make_async_copy(hid_mine.at[rep], hid_out.at[:, mine], sem_local.at[3])
    keep_hid.start()

    for n, k in enumerate(back_order):
        if k:
            back_sends[n_rep - k - 1].wait_recv()

        @pl.loop(0, per)
        def _(q, n=n, k=k):
            chunk = (rep + k) % n_rep
            lhs = back[chunk, q]
            for s in range(0, n_slot, BACK_GROUP):
                some = dot(lhs, join([tiles[chunk * per + q, s + t] for t in range(BACK_GROUP)]), NN)
                for u in range(BACK_GROUP):
                    t = (n * per + q) * n_slot + s + u
                    run[t] = some[:, u * TILE:(u + 1) * TILE] + run[table_s[1, t]]

    part_sends = {}
    for g in far_first:
        for b in range(n_blk):
            part[g, b] = run[table_s[2, g * n_blk + b]].astype(BF16)
        part_sends[g] = send(
            part.at[g], part_in.at[g], ss_part.at[g], rs_part.at[g], row_at(offsets[g])
        )
        if g != FAR:
            part_sends[g].start()

    for c in team_sends:
        c.wait_recv()
    s3_mine[0:9, :] = sum(team_in[k, m, 0:9] for k in range(n_rep) for m in range(plane))
    s3_sends = []
    for k in layers:
        c = send(s3_mine.at[0:9], s3_in.at[layer, 0:9], ss_s3.at[k - 1], rs_s3.at[k - 1], layer_at(k))
        c.start()
        s3_sends.append(c)
    part_sends[FAR].start()
    s3_in[layer, 0:9] = s3_mine[0:9, :]
    for c in s3_sends:
        c.wait_recv()
    done = sum(s3_in[m, 0:9] for m in range(depth))
    gw_mine[...] = done[0:8, :]
    gb_mine[...] = jnp.broadcast_to(done[8:9, :], gb_mine.shape)
    keep_gb = pltpu.make_async_copy(gb_mine, gb_out, sem_local.at[5])
    keep_gb.start()
    my_rows = pl.ds(pl.multiple_of(spot * 8, 8), 8)
    s4_sends = []
    for k in spots:
        c = send(gw_mine, gw_out.at[my_rows, :], ss_s4.at[k - 1], rs_s4.at[k - 1], spot_at(k))
        c.start()
        s4_sends.append(c)
    keep_gw = pltpu.make_async_copy(gw_mine, gw_out.at[my_rows, :], sem_local.at[4])
    keep_gw.start()

    for g in far_first:
        part_sends[g].wait_recv()
    for b in range(n_blk):
        value = run[table_s[2, OWN * n_blk + b]]
        for g in far_first:
            value += part_in[g, b].astype(F32)
        gf_mine[:, b * TILE:(b + 1) * TILE] = value.astype(BF16)
    keep_gf = pltpu.make_async_copy(gf_mine, gf_out, sem_local.at[2])
    keep_gf.start()

    for c in hid_sends + s4_sends:
        c.wait_recv()
    keep_hid.wait()
    keep_gw.wait()
    keep_gb.wait()
    keep_gf.wait()
    everything = [feat_sends[g] for g in far_first] + pre_sends + agg_sends + back_sends + hid_sends
    everything += team_sends + s3_sends + s4_sends + [part_sends[g] for g in far_first]
    for c in everything:
        c.wait_send()


def finish(hid_in, gw_in, gb_in, gf_in, hid_out, gw_out, gb_out, gf_out, hid, gw, gb, gf, sems):
    through = ((hid_in, hid, hid_out), (gf_in, gf, gf_out), (gw_in, gw, gw_out))
    loads = [pltpu.make_async_copy(a, b, sems.at[0, n]) for n, (a, b, c) in enumerate(through)]
    loads.append(pltpu.make_async_copy(gb_in, gb, sems.at[0, 3]))
    stores = [pltpu.make_async_copy(b, c, sems.at[1, n]) for n, (a, b, c) in enumerate(through)]
    for c in loads:
        c.start()
    for n, c in enumerate(stores):
        loads[n].wait()
        c.start()
    loads[3].wait()
    gb_out[...] = gb[0:1, 0:gb_out.shape[1]]
    for c in stores:
        c.wait()


def body(n_row, n_rep, plane, features, tiles, tile_cols, counts, weight, bias, cotangent):
    n_blk, n_slot = tiles.shape[:2]
    rows, width = features.shape
    n_hid = weight.shape[1]
    fin = weight.shape[0]
    span = rows // n_rep
    depth = n_row // plane
    n_far = len(OFFSETS)
    n_slots = n_blk * n_slot
    dma = pltpu.SemaphoreType.DMA
    vmem = pl.BlockSpec(memory_space=pltpu.VMEM)
    smem = pl.BlockSpec(memory_space=pltpu.SMEM)
    hbm = pl.BlockSpec(memory_space=pltpu.HBM)

    def pair(*shape):
        return [dma(shape), dma(shape)]

    out = pl.pallas_call(
        functools.partial(kernel, n_row, n_rep, plane),
        out_shape=(
            jax.ShapeDtypeStruct((n_hid, rows), BF16),
            jax.ShapeDtypeStruct((n_hid, fin), F32),
            jax.ShapeDtypeStruct((8, TILE), F32),
            jax.ShapeDtypeStruct((width, rows), BF16),
        ),
        in_specs=[hbm] * 7,
        out_specs=(hbm, hbm, hbm, hbm),
        scratch_shapes=[
            pltpu.VMEM(tile_cols.shape, jnp.int32),
            pltpu.SMEM(counts.shape, jnp.int32),
            pltpu.VMEM((1, n_hid), F32),
            pltpu.VMEM(tiles.shape, BF16),
            pltpu.VMEM((len(OFFSETS) * n_blk + 1, width, TILE), BF16),
            pltpu.VMEM((n_rep, n_hid, span), BF16),
            pltpu.VMEM((n_rep, n_hid, fin), BF16),
            pltpu.VMEM((n_rep, 8, TILE), F32),
            pltpu.VMEM((fin, n_rep * n_hid), BF16),
            pltpu.VMEM((n_rep, n_hid, TILE), F32),
            pltpu.VMEM((n_blk, TILE), jnp.int32),
            pltpu.VMEM((8, TILE), jnp.int32),
            pltpu.SMEM((8, TILE), jnp.int32),
            pltpu.VMEM((n_rep, n_blk // n_rep, width, TILE), BF16),
            pltpu.VMEM((n_rep, n_blk // n_rep, width, TILE), BF16),
            pltpu.VMEM((n_rep, n_hid, span), BF16),
            pltpu.VMEM((n_rep, n_hid, span), BF16),
            pltpu.VMEM((n_rep, n_blk // n_rep, width, TILE), BF16),
            pltpu.VMEM((n_rep, n_blk // n_rep, width, TILE), BF16),
            pltpu.VMEM((n_slots + 1, width, TILE), F32),
            pltpu.VMEM((n_far, n_blk, width, TILE), BF16),
            pltpu.VMEM((n_far, n_blk, width, TILE), BF16),
            pltpu.VMEM((n_rep, plane, 16, TILE), F32),
            pltpu.VMEM((n_rep, plane, 16, TILE), F32),
            pltpu.VMEM((16, TILE), F32),
            pltpu.VMEM((depth, 16, TILE), F32),
            pltpu.VMEM((8, TILE), F32),
            pltpu.VMEM((8, TILE), F32),
            pltpu.VMEM((width, rows), BF16),
            dma((n_blk,)),
            dma((n_rep,)),
            dma((8,)),
            *pair(n_far),
            *pair(3, n_rep - 1),
            *pair(n_rep - 1),
            *pair(n_rep - 1),
            *pair(n_rep - 1),
            *pair(n_rep * plane - 1),
            *pair(depth - 1),
            *pair(plane - 1),
            *pair(n_far),
        ],
        compiler_params=pltpu.CompilerParams(
            collective_id=0, has_side_effects=True, vmem_limit_bytes=62 * 1024 * 1024
        ),
        cost_estimate=pl.CostEstimate(
            flops=4 * n_slots * TILE * TILE * width, bytes_accessed=tiles.size * 2, transcendentals=span * n_rep * n_hid
        ),
    )(
        tile_cols, counts, bias.reshape(1, n_hid), features.T, tiles, weight.T, cotangent.T,
    )
    hidden, grad_weight, grad_bias, grad_features = pl.pallas_call(
        finish,
        out_shape=(
            jax.ShapeDtypeStruct((n_hid, rows), BF16),
            jax.ShapeDtypeStruct((n_hid, fin), F32),
            jax.ShapeDtypeStruct((1, n_hid), F32),
            jax.ShapeDtypeStruct((width, rows), BF16),
        ),
        in_specs=[hbm] * 4,
        out_specs=(hbm, hbm, vmem, hbm),
        scratch_shapes=[
            pltpu.VMEM((n_hid, rows), BF16),
            pltpu.VMEM((n_hid, fin), F32),
            pltpu.VMEM((8, TILE), F32),
            pltpu.VMEM((width, rows), BF16),
            dma((2, 4)),
        ],
        compiler_params=pltpu.CompilerParams(vmem_limit_bytes=62 * 1024 * 1024),
    )(*out)
    return hidden.T, grad_weight.T, grad_bias.reshape(n_hid), grad_features.T


def solution(mesh):
    in_specs = (
        P("row", "rep"),
        P("row", None, None, None),
        P("row", None),
        P("row"),
        P(None, "rep"),
        P("rep"),
        P("row", "rep"),
    )
    out_specs = (P("row", "rep"), P(None, "rep"), P("rep"), P("row", "rep"))
    n_row, n_rep = mesh.shape["row"], mesh.shape["rep"]
    step = functools.partial(body, n_row, n_rep, 8)
    return jax.shard_map(step, mesh=mesh, in_specs=in_specs, out_specs=out_specs, check_vma=False)
```

```python
import functools

import jax
import jax.numpy as jnp
from jax import lax
from jax.experimental import pallas as pl
from jax.experimental.pallas import tpu as pltpu
from jax.sharding import PartitionSpec as P

F32 = jnp.float32
BF16 = jnp.bfloat16
TILE = 128
OFFSETS = (-2, -1, 0, 1, 2, None)
OWN = 2
FAR = 5
GROUP = 2
BACK_GROUP = 2
NT = (((1,), (1,)), ((), ()))
NN = (((1,), (0,)), ((), ()))


def dot(a, b, dims):
    return lax.dot_general(a, b, dims, preferred_element_type=F32)


def join(parts):
    return jnp.concatenate(parts, axis=1) if len(parts) > 1 else parts[0]


def kernel(
    n_row, n_rep, plane,
    cols_hbm, counts_hbm, bias_hbm, ft_ref, tiles_ref, wt_ref, ct_ref,
    hid_out, gw_out, gb_out, gf_out,
    cols_ref, counts_ref, bias_ref, tiles, feats, cots, weights, biases, weight_fh, bias_col, keys_2d, table, table_s,
    agg_mine, agg, hid_mine, delta, back_mine, back, run, part, part_in,
    team_mine, team_in, s3_mine, s3_in, gw_mine, gb_mine, gf_mine,
    sem_feat, sem_tile, sem_local,
    ss_feat, rs_feat, ss_pre, rs_pre, ss_agg, rs_agg, ss_back, rs_back, ss_hid, rs_hid,
    ss_team, rs_team, ss_s3, rs_s3, ss_s4, rs_s4, ss_part, rs_part,
):
    row = lax.axis_index("row")
    rep = lax.axis_index("rep")
    depth = n_row // plane
    layer = row // plane
    spot = row % plane
    n_blk = tiles_ref.shape[0]
    n_slot = tiles_ref.shape[1]
    per = n_blk // n_rep
    span = per * TILE
    none_feat = len(OFFSETS) * n_blk
    n_slots = n_blk * n_slot
    offsets = [n_row // 2 if o is None else o for o in OFFSETS]
    far_first = (5, 0, 4, 1, 3)
    feat_order = (0, 5, 4, 1, 3)
    hops = [min(k, n_rep - k) for k in range(n_rep)]
    near_last = sorted(range(1, n_rep), key=lambda k: -hops[k])
    order = near_last + [0]
    team = [(k, m) for k in range(n_rep) for m in range(plane) if (k, m) != (0, 0)]
    team.sort(key=lambda o: -hops[o[0]] - min(o[1], plane - o[1]) / 2)
    spots = sorted(range(1, plane), key=lambda m: -min(m, plane - m))
    layers = sorted(range(1, depth), key=lambda m: -min(m, depth - m))
    back_order = [0] + near_last[::-1]

    def block_at(p, q=0):
        return ((rep + back_order[p // per]) % n_rep) * per + p % per + q

    def row_at(offset):
        return {"row": (row + offset + n_row) % n_row, "rep": rep}

    def rep_at(k):
        return {"row": row, "rep": (rep + k) % n_rep}

    def team_at(k, m):
        return {"row": layer * plane + (spot + m) % plane, "rep": (rep + k) % n_rep}

    def spot_at(k):
        return {"row": layer * plane + (spot + k) % plane, "rep": rep}

    def layer_at(k):
        return {"row": ((layer + k) % depth) * plane + spot, "rep": rep}

    def send(src, dst, ss, rs, where):
        return pltpu.make_async_remote_copy(
            src_ref=src, dst_ref=dst, send_sem=ss, recv_sem=rs,
            device_id=where, device_id_type=pl.DeviceIdType.MESH,
        )

    barrier = pltpu.get_barrier_semaphore()
    peers = [row_at(offsets[g]) for g in far_first]
    peers += [team_at(*o) for o in team]
    peers += [layer_at(k) for k in layers]
    for where in peers:
        pl.semaphore_signal(barrier, inc=1, device_id=where, device_id_type=pl.DeviceIdType.MESH)

    feat_loads = [
        pltpu.make_async_copy(ft_ref.at[:, TILE * b:TILE * (b + 1)], feats.at[OWN * n_blk + b], sem_feat.at[b])
        for b in range(n_blk)
    ]
    for c in feat_loads:
        c.start()
    mine = pl.ds(pl.multiple_of(rep * span, span), span)
    load_w = pltpu.make_async_copy(wt_ref, weights.at[rep], sem_local.at[0])
    load_c = pltpu.make_async_copy(ct_ref.at[:, mine], cots.at[rep], sem_local.at[1])
    load_cols = pltpu.make_async_copy(cols_hbm, cols_ref, sem_local.at[5])
    load_counts = pltpu.make_async_copy(counts_hbm, counts_ref, sem_local.at[6])
    load_bias = pltpu.make_async_copy(bias_hbm, bias_ref, sem_local.at[7])
    for c in (load_w, load_bias, load_cols, load_counts, load_c):
        c.start()
    tile_loads = []
    for k in range(n_rep):
        which = pl.ds(((rep + k) % n_rep) * per, per)
        tile_loads.append(
            pltpu.make_async_copy(tiles_ref.at[which], tiles.at[which], sem_tile.at[k])
        )
    for k in order:
        tile_loads[k].start()

    pl.semaphore_wait(barrier, len(peers))

    for c in feat_loads:
        c.wait()
    feat_sends = {
        g: send(
            feats.at[OWN * n_blk:(OWN + 1) * n_blk], feats.at[g * n_blk:(g + 1) * n_blk],
            ss_feat.at[g], rs_feat.at[g], row_at(-offsets[g]),
        )
        for g in far_first
    }
    for g in feat_order:
        feat_sends[g].start()
    load_w.wait()
    load_bias.wait()
    biases[rep] = jnp.broadcast_to(jnp.pad(bias_ref[...], ((0, 0), (0, TILE - bias_ref.shape[1]))), (8, TILE))
    pre_sends = []
    for k in range(1, n_rep):
        pre_sends.append(send(weights.at[rep], weights.at[rep], ss_pre.at[0, k - 1], rs_pre.at[0, k - 1], rep_at(k)))
        pre_sends.append(send(biases.at[rep], biases.at[rep], ss_pre.at[1, k - 1], rs_pre.at[1, k - 1], rep_at(k)))
        pre_sends.append(
            send(
                ct_ref.at[:, pl.ds(pl.multiple_of(((rep + k) % n_rep) * span, span), span)],
                cots.at[rep], ss_pre.at[2, k - 1], rs_pre.at[2, k - 1], rep_at(k),
            )
        )
    for c in pre_sends:
        c.start()

    load_cols.wait()
    load_counts.wait()
    cols = cols_ref[...]
    shape = cols.shape
    slot = lax.broadcasted_iota(jnp.int32, shape, 1)
    line = lax.broadcasted_iota(jnp.int32, shape, 0)
    count = jnp.zeros(shape, jnp.int32)
    for i in range(n_blk):
        count = jnp.where(line == i, counts_ref[i], count)
    group = jnp.minimum((cols // n_blk - row + 2 + n_row) % n_row, 5)
    key = jnp.where(slot < count, group * n_blk + cols % n_blk, none_feat)
    keys_2d[:, 0:n_slot] = key
    keys = jnp.concatenate([keys_2d[pl.ds(block_at(p), 1), 0:n_slot] for p in range(n_blk)], axis=1)
    by_lane = jnp.broadcast_to(keys, (n_slots, n_slots))
    by_line = by_lane.T
    up = lax.broadcasted_iota(jnp.int32, (n_slots, n_slots), 0)
    across = lax.broadcasted_iota(jnp.int32, (n_slots, n_slots), 1)
    before = jnp.max(jnp.where((by_line == by_lane) & (up < across), up, -1), axis=0, keepdims=True)
    last = jnp.max(jnp.where(by_line == across, up, -1), axis=0, keepdims=True)
    table[0:1, :] = keys
    table[1:2, :] = jnp.where(before < 0, n_slots, before)
    table[2:3, :] = jnp.where(last < 0, n_slots, last)
    table[3:8, :] = jnp.zeros((5, n_slots), jnp.int32)
    to_scalar = pltpu.make_async_copy(table, table_s, sem_local.at[2])
    to_scalar.start()
    feats[none_feat] = jnp.zeros(feats.shape[1:], BF16)
    run[n_slots] = jnp.zeros(run.shape[1:], F32)
    to_scalar.wait()

    for g in far_first:
        feat_sends[g].wait_recv()

    agg_sends = []
    for k in order:
        tile_loads[k].wait()

        @pl.loop(0, per)
        def _(q, k=k):
            p = back_order.index(k) * per + q
            i = ((rep + k) % n_rep) * per + q
            total = jnp.zeros((feats.shape[1], TILE), F32)
            for s in range(0, n_slot, GROUP):
                some = [feats[table_s[0, p * n_slot + s + t]] for t in range(GROUP)]
                total += dot(join(some), join([tiles[i, s + t] for t in range(GROUP)]), NT)
            agg_mine[k, q] = total.astype(BF16)

        if k:
            c = send(agg_mine.at[k], agg.at[rep], ss_agg.at[k - 1], rs_agg.at[k - 1], rep_at(k))
            c.start()
            agg_sends.append(c)
    agg[rep] = agg_mine[0]

    for c in pre_sends:
        c.wait_recv()
    load_c.wait()
    n_hid = weights.shape[1]
    for j in range(n_rep):
        weight_fh[:, j * n_hid:(j + 1) * n_hid] = weights[j].astype(F32).T.astype(BF16)
        bias_col[j] = jnp.broadcast_to(biases[j, 0:1, :], (TILE, TILE)).T[0:n_hid, :]

    for c in agg_sends:
        c.wait_recv()

    width = agg.shape[2]
    whole = jnp.concatenate([agg[:, q].reshape(n_rep * width, TILE) for q in range(per)], axis=1)
    hid_sends = []
    for j in range(n_rep):
        wide_bias = jnp.concatenate([bias_col[j]] * (span // TILE), axis=1)
        pre = dot(weights[j], whole, NN) + wide_bias
        sigma = jax.nn.sigmoid(pre)
        hid_mine[j] = (pre * sigma).astype(BF16)
        delta[j] = (cots[j].astype(F32) * sigma * (1.0 + pre * (1.0 - sigma))).astype(BF16)
    deltas = delta[...].reshape(n_rep * n_hid, span)
    back_full = dot(weight_fh[...], deltas, NN).astype(BF16)
    for q in range(per):
        back_mine[:, q] = back_full[:, q * TILE:(q + 1) * TILE].reshape(n_rep, width, TILE)
    ones = jnp.ones((8, span), BF16)
    team_sends = []
    for j in range(n_rep):
        grad = dot(delta[j], whole, NT)
        bias_grad = jnp.pad(dot(ones, delta[j], NT)[0:1, :], ((0, 0), (0, TILE - n_hid)))
        for m in range(plane):
            team_mine[j, m, 0:8, :] = grad[8 * m:8 * (m + 1), :]
            team_mine[j, m, 8:9, :] = bias_grad
    back_sends = []
    for k in range(1, n_rep):
        c = send(back_mine.at[(rep + k) % n_rep], back.at[rep], ss_back.at[k - 1], rs_back.at[k - 1], rep_at(k))
        c.start()
        back_sends.append(c)
    back[rep] = back_mine[rep]
    for n, (k, m) in enumerate(team):
        c = send(
            team_mine.at[(rep + k) % n_rep, (spot + m) % plane, 0:9], team_in.at[rep, spot, 0:9],
            ss_team.at[n], rs_team.at[n], team_at(k, m),
        )
        c.start()
        team_sends.append(c)
    team_in[rep, spot, 0:9] = team_mine[rep, spot, 0:9]
    for n, k in enumerate(back_order):
        if k:
            back_sends[n_rep - k - 1].wait_recv()

        @pl.loop(0, per)
        def _(q, n=n, k=k):
            chunk = (rep + k) % n_rep
            lhs = back[chunk, q]
            for s in range(0, n_slot, BACK_GROUP):
                some = dot(lhs, join([tiles[chunk * per + q, s + t] for t in range(BACK_GROUP)]), NN)
                for u in range(BACK_GROUP):
                    t = (n * per + q) * n_slot + s + u
                    run[t] = some[:, u * TILE:(u + 1) * TILE] + run[table_s[1, t]]

    for c in team_sends:
        c.wait_recv()
    s3_mine[0:9, :] = sum(team_in[k, m, 0:9] for k in range(n_rep) for m in range(plane))
    s3_sends = []
    for k in layers:
        c = send(s3_mine.at[0:9], s3_in.at[layer, 0:9], ss_s3.at[k - 1], rs_s3.at[k - 1], layer_at(k))
        c.start()
        s3_sends.append(c)
    part_sends = {}
    for g in far_first:
        for b in range(n_blk):
            part[g, b] = run[table_s[2, g * n_blk + b]].astype(BF16)
        part_sends[g] = send(
            part.at[g], part_in.at[g], ss_part.at[g], rs_part.at[g], row_at(offsets[g])
        )
        part_sends[g].start()

    s3_in[layer, 0:9] = s3_mine[0:9, :]
    for k in range(1, n_rep):
        c = send(hid_mine.at[(rep + k) % n_rep], hid_out.at[:, mine], ss_hid.at[k - 1], rs_hid.at[k - 1], rep_at(k))
        c.start()
        hid_sends.append(c)
    keep_hid = pltpu.make_async_copy(hid_mine.at[rep], hid_out.at[:, mine], sem_local.at[3])
    keep_hid.start()

    for c in s3_sends:
        c.wait_recv()
    done = sum(s3_in[m, 0:9] for m in range(depth))
    gw_mine[...] = done[0:8, :]
    gb_mine[...] = jnp.broadcast_to(done[8:9, :], gb_mine.shape)
    keep_gb = pltpu.make_async_copy(gb_mine, gb_out, sem_local.at[5])
    keep_gb.start()
    my_rows = pl.ds(pl.multiple_of(spot * 8, 8), 8)
    s4_sends = []
    for k in spots:
        c = send(gw_mine, gw_out.at[my_rows, :], ss_s4.at[k - 1], rs_s4.at[k - 1], spot_at(k))
        c.start()
        s4_sends.append(c)
    keep_gw = pltpu.make_async_copy(gw_mine, gw_out.at[my_rows, :], sem_local.at[4])
    keep_gw.start()

    for g in far_first:
        part_sends[g].wait_recv()
    for b in range(n_blk):
        value = run[table_s[2, OWN * n_blk + b]]
        for g in far_first:
            value += part_in[g, b].astype(F32)
        gf_mine[:, b * TILE:(b + 1) * TILE] = value.astype(BF16)
    keep_gf = pltpu.make_async_copy(gf_mine, gf_out, sem_local.at[2])
    keep_gf.start()

    for c in hid_sends + s4_sends:
        c.wait_recv()
    keep_hid.wait()
    keep_gw.wait()
    keep_gb.wait()
    keep_gf.wait()
    everything = [feat_sends[g] for g in far_first] + pre_sends + agg_sends + back_sends + hid_sends
    everything += team_sends + s3_sends + s4_sends + [part_sends[g] for g in far_first]
    for c in everything:
        c.wait_send()


def finish(hid_in, gw_in, gb_in, gf_in, hid_out, gw_out, gb_out, gf_out, hid, gw, gb, gf, sems):
    through = ((hid_in, hid, hid_out), (gf_in, gf, gf_out), (gw_in, gw, gw_out))
    loads = [pltpu.make_async_copy(a, b, sems.at[0, n]) for n, (a, b, c) in enumerate(through)]
    loads.append(pltpu.make_async_copy(gb_in, gb, sems.at[0, 3]))
    stores = [pltpu.make_async_copy(b, c, sems.at[1, n]) for n, (a, b, c) in enumerate(through)]
    for c in loads:
        c.start()
    for n, c in enumerate(stores):
        loads[n].wait()
        c.start()
    loads[3].wait()
    gb_out[...] = gb[0:1, 0:gb_out.shape[1]]
    for c in stores:
        c.wait()


def body(n_row, n_rep, plane, features, tiles, tile_cols, counts, weight, bias, cotangent):
    n_blk, n_slot = tiles.shape[:2]
    rows, width = features.shape
    n_hid = weight.shape[1]
    fin = weight.shape[0]
    span = rows // n_rep
    depth = n_row // plane
    n_far = len(OFFSETS)
    n_slots = n_blk * n_slot
    dma = pltpu.SemaphoreType.DMA
    vmem = pl.BlockSpec(memory_space=pltpu.VMEM)
    smem = pl.BlockSpec(memory_space=pltpu.SMEM)
    hbm = pl.BlockSpec(memory_space=pltpu.HBM)

    def pair(*shape):
        return [dma(shape), dma(shape)]

    out = pl.pallas_call(
        functools.partial(kernel, n_row, n_rep, plane),
        out_shape=(
            jax.ShapeDtypeStruct((n_hid, rows), BF16),
            jax.ShapeDtypeStruct((n_hid, fin), F32),
            jax.ShapeDtypeStruct((8, TILE), F32),
            jax.ShapeDtypeStruct((width, rows), BF16),
        ),
        in_specs=[hbm] * 7,
        out_specs=(hbm, hbm, hbm, hbm),
        scratch_shapes=[
            pltpu.VMEM(tile_cols.shape, jnp.int32),
            pltpu.SMEM(counts.shape, jnp.int32),
            pltpu.VMEM((1, n_hid), F32),
            pltpu.VMEM(tiles.shape, BF16),
            pltpu.VMEM((len(OFFSETS) * n_blk + 1, width, TILE), BF16),
            pltpu.VMEM((n_rep, n_hid, span), BF16),
            pltpu.VMEM((n_rep, n_hid, fin), BF16),
            pltpu.VMEM((n_rep, 8, TILE), F32),
            pltpu.VMEM((fin, n_rep * n_hid), BF16),
            pltpu.VMEM((n_rep, n_hid, TILE), F32),
            pltpu.VMEM((n_blk, TILE), jnp.int32),
            pltpu.VMEM((8, TILE), jnp.int32),
            pltpu.SMEM((8, TILE), jnp.int32),
            pltpu.VMEM((n_rep, n_blk // n_rep, width, TILE), BF16),
            pltpu.VMEM((n_rep, n_blk // n_rep, width, TILE), BF16),
            pltpu.VMEM((n_rep, n_hid, span), BF16),
            pltpu.VMEM((n_rep, n_hid, span), BF16),
            pltpu.VMEM((n_rep, n_blk // n_rep, width, TILE), BF16),
            pltpu.VMEM((n_rep, n_blk // n_rep, width, TILE), BF16),
            pltpu.VMEM((n_slots + 1, width, TILE), F32),
            pltpu.VMEM((n_far, n_blk, width, TILE), BF16),
            pltpu.VMEM((n_far, n_blk, width, TILE), BF16),
            pltpu.VMEM((n_rep, plane, 16, TILE), F32),
            pltpu.VMEM((n_rep, plane, 16, TILE), F32),
            pltpu.VMEM((16, TILE), F32),
            pltpu.VMEM((depth, 16, TILE), F32),
            pltpu.VMEM((8, TILE), F32),
            pltpu.VMEM((8, TILE), F32),
            pltpu.VMEM((width, rows), BF16),
            dma((n_blk,)),
            dma((n_rep,)),
            dma((8,)),
            *pair(n_far),
            *pair(3, n_rep - 1),
            *pair(n_rep - 1),
            *pair(n_rep - 1),
            *pair(n_rep - 1),
            *pair(n_rep * plane - 1),
            *pair(depth - 1),
            *pair(plane - 1),
            *pair(n_far),
        ],
        compiler_params=pltpu.CompilerParams(
            collective_id=0, has_side_effects=True, vmem_limit_bytes=62 * 1024 * 1024
        ),
        cost_estimate=pl.CostEstimate(
            flops=4 * n_slots * TILE * TILE * width, bytes_accessed=tiles.size * 2, transcendentals=span * n_rep * n_hid
        ),
    )(
        tile_cols, counts, bias.reshape(1, n_hid), features.T, tiles, weight.T, cotangent.T,
    )
    hidden, grad_weight, grad_bias, grad_features = pl.pallas_call(
        finish,
        out_shape=(
            jax.ShapeDtypeStruct((n_hid, rows), BF16),
            jax.ShapeDtypeStruct((n_hid, fin), F32),
            jax.ShapeDtypeStruct((1, n_hid), F32),
            jax.ShapeDtypeStruct((width, rows), BF16),
        ),
        in_specs=[hbm] * 4,
        out_specs=(hbm, hbm, vmem, hbm),
        scratch_shapes=[
            pltpu.VMEM((n_hid, rows), BF16),
            pltpu.VMEM((n_hid, fin), F32),
            pltpu.VMEM((8, TILE), F32),
            pltpu.VMEM((width, rows), BF16),
            dma((2, 4)),
        ],
        compiler_params=pltpu.CompilerParams(vmem_limit_bytes=62 * 1024 * 1024),
    )(*out)
    return hidden.T, grad_weight.T, grad_bias.reshape(n_hid), grad_features.T


def solution(mesh):
    in_specs = (
        P("row", "rep"),
        P("row", None, None, None),
        P("row", None),
        P("row"),
        P(None, "rep"),
        P("rep"),
        P("row", "rep"),
    )
    out_specs = (P("row", "rep"), P(None, "rep"), P("rep"), P("row", "rep"))
    n_row, n_rep = mesh.shape["row"], mesh.shape["rep"]
    step = functools.partial(body, n_row, n_rep, 8)
    return jax.shard_map(step, mesh=mesh, in_specs=in_specs, out_specs=out_specs, check_vma=False)
```

```python
import functools

import jax
import jax.numpy as jnp
from jax import lax
from jax.experimental import pallas as pl
from jax.experimental.pallas import tpu as pltpu
from jax.sharding import PartitionSpec as P

F32 = jnp.float32
BF16 = jnp.bfloat16
TILE = 128
OFFSETS = (-2, -1, 0, 1, 2, None)
OWN = 2
FAR = 5
GROUP = 2
BACK_GROUP = 2
NT = (((1,), (1,)), ((), ()))
NN = (((1,), (0,)), ((), ()))


def dot(a, b, dims):
    return lax.dot_general(a, b, dims, preferred_element_type=F32)


def join(parts):
    return jnp.concatenate(parts, axis=1) if len(parts) > 1 else parts[0]


def kernel(
    n_row, n_rep, plane,
    cols_hbm, counts_hbm, bias_hbm, ft_ref, tiles_ref, wt_ref, ct_ref,
    hid_out, gw_out, gb_out, gf_out,
    cols_ref, counts_ref, bias_ref, tiles, feats, cots, weights, biases, weight_fh, bias_col, keys_2d, table, table_s,
    agg_mine, agg, hid_mine, delta, back_mine, back, run, part, part_in,
    team_mine, team_in, s3_mine, s3_in, gw_mine, gb_mine, gf_mine,
    sem_feat, sem_tile, sem_local,
    ss_feat, rs_feat, ss_pre, rs_pre, ss_agg, rs_agg, ss_back, rs_back, ss_hid, rs_hid,
    ss_team, rs_team, ss_s3, rs_s3, ss_s4, rs_s4, ss_part, rs_part,
):
    row = lax.axis_index("row")
    rep = lax.axis_index("rep")
    depth = n_row // plane
    layer = row // plane
    spot = row % plane
    n_blk = tiles_ref.shape[0]
    n_slot = tiles_ref.shape[1]
    per = n_blk // n_rep
    span = per * TILE
    none_feat = len(OFFSETS) * n_blk
    n_slots = n_blk * n_slot
    offsets = [n_row // 2 if o is None else o for o in OFFSETS]
    far_first = (5, 0, 4, 1, 3)
    feat_order = (0, 4, 5, 1, 3)
    hops = [min(k, n_rep - k) for k in range(n_rep)]
    near_last = sorted(range(1, n_rep), key=lambda k: -hops[k])
    order = near_last + [0]
    n_x = plane // 2
    chip = spot // 2
    core = spot % 2
    team = [(k, m) for k in range(n_rep) for m in range(n_x) if (k, m) != (0, 0)]
    team.sort(key=lambda o: -hops[o[0]] - min(o[1], n_x - o[1]))
    column = [(k, c) for k in range(depth) for c in range(2) if (k, c) != (0, 0)]
    column.sort(key=lambda o: -min(o[0], depth - o[0]))
    chips = sorted(range(1, n_x), key=lambda m: -min(m, n_x - m))
    back_order = [0] + near_last[::-1]

    def block_at(p, q=0):
        return ((rep + back_order[p // per]) % n_rep) * per + p % per + q

    def row_at(offset):
        return {"row": (row + offset + n_row) % n_row, "rep": rep}

    def rep_at(k):
        return {"row": row, "rep": (rep + k) % n_rep}

    def team_at(k, m):
        return {"row": layer * plane + (chip + m) % n_x * 2 + core, "rep": (rep + k) % n_rep}

    def column_at(k, c):
        return {"row": (layer + k) % depth * plane + chip * 2 + (core + c) % 2, "rep": rep}

    def send(src, dst, ss, rs, where):
        return pltpu.make_async_remote_copy(
            src_ref=src, dst_ref=dst, send_sem=ss, recv_sem=rs,
            device_id=where, device_id_type=pl.DeviceIdType.MESH,
        )

    barrier = pltpu.get_barrier_semaphore()
    peers = [row_at(offsets[g]) for g in far_first]
    peers += [team_at(*o) for o in team]
    peers += [column_at(*o) for o in column]
    for where in peers:
        pl.semaphore_signal(barrier, inc=1, device_id=where, device_id_type=pl.DeviceIdType.MESH)

    feat_loads = [
        pltpu.make_async_copy(ft_ref.at[:, TILE * b:TILE * (b + 1)], feats.at[OWN * n_blk + b], sem_feat.at[b])
        for b in range(n_blk)
    ]
    for c in feat_loads:
        c.start()
    mine = pl.ds(pl.multiple_of(rep * span, span), span)
    load_w = pltpu.make_async_copy(wt_ref, weights.at[rep], sem_local.at[0])
    load_c = pltpu.make_async_copy(ct_ref.at[:, mine], cots.at[rep], sem_local.at[1])
    load_cols = pltpu.make_async_copy(cols_hbm, cols_ref, sem_local.at[5])
    load_counts = pltpu.make_async_copy(counts_hbm, counts_ref, sem_local.at[6])
    load_bias = pltpu.make_async_copy(bias_hbm, bias_ref, sem_local.at[7])
    for c in (load_w, load_bias, load_cols, load_counts, load_c):
        c.start()
    tile_loads = []
    for k in range(n_rep):
        which = pl.ds(((rep + k) % n_rep) * per, per)
        tile_loads.append(
            pltpu.make_async_copy(tiles_ref.at[which], tiles.at[which], sem_tile.at[k])
        )
    for k in order:
        tile_loads[k].start()

    pl.semaphore_wait(barrier, len(peers))

    for c in feat_loads:
        c.wait()
    feat_sends = {
        g: send(
            feats.at[OWN * n_blk:(OWN + 1) * n_blk], feats.at[g * n_blk:(g + 1) * n_blk],
            ss_feat.at[g], rs_feat.at[g], row_at(-offsets[g]),
        )
        for g in far_first
    }
    for g in feat_order:
        feat_sends[g].start()
    load_w.wait()
    load_bias.wait()
    biases[rep] = jnp.broadcast_to(jnp.pad(bias_ref[...], ((0, 0), (0, TILE - bias_ref.shape[1]))), (8, TILE))
    pre_sends = []
    for k in range(1, n_rep):
        pre_sends.append(send(weights.at[rep], weights.at[rep], ss_pre.at[0, k - 1], rs_pre.at[0, k - 1], rep_at(k)))
        pre_sends.append(send(biases.at[rep], biases.at[rep], ss_pre.at[1, k - 1], rs_pre.at[1, k - 1], rep_at(k)))
        pre_sends.append(
            send(
                ct_ref.at[:, pl.ds(pl.multiple_of(((rep + k) % n_rep) * span, span), span)],
                cots.at[rep], ss_pre.at[2, k - 1], rs_pre.at[2, k - 1], rep_at(k),
            )
        )
    for c in pre_sends:
        c.start()

    load_cols.wait()
    load_counts.wait()
    cols = cols_ref[...]
    shape = cols.shape
    slot = lax.broadcasted_iota(jnp.int32, shape, 1)
    line = lax.broadcasted_iota(jnp.int32, shape, 0)
    count = jnp.zeros(shape, jnp.int32)
    for i in range(n_blk):
        count = jnp.where(line == i, counts_ref[i], count)
    group = jnp.minimum((cols // n_blk - row + 2 + n_row) % n_row, 5)
    key = jnp.where(slot < count, group * n_blk + cols % n_blk, none_feat)
    keys_2d[:, 0:n_slot] = key
    keys = jnp.concatenate([keys_2d[pl.ds(block_at(p), 1), 0:n_slot] for p in range(n_blk)], axis=1)
    by_lane = jnp.broadcast_to(keys, (n_slots, n_slots))
    by_line = by_lane.T
    up = lax.broadcasted_iota(jnp.int32, (n_slots, n_slots), 0)
    across = lax.broadcasted_iota(jnp.int32, (n_slots, n_slots), 1)
    before = jnp.max(jnp.where((by_line == by_lane) & (up < across), up, -1), axis=0, keepdims=True)
    last = jnp.max(jnp.where(by_line == across, up, -1), axis=0, keepdims=True)
    table[0:1, :] = keys
    table[1:2, :] = jnp.where(before < 0, n_slots, before)
    table[2:3, :] = jnp.where(last < 0, n_slots, last)
    table[3:8, :] = jnp.zeros((5, n_slots), jnp.int32)
    to_scalar = pltpu.make_async_copy(table, table_s, sem_local.at[2])
    to_scalar.start()
    feats[none_feat] = jnp.zeros(feats.shape[1:], BF16)
    run[n_slots] = jnp.zeros(run.shape[1:], F32)
    to_scalar.wait()

    for g in far_first:
        feat_sends[g].wait_recv()

    agg_sends = []
    for k in order:
        tile_loads[k].wait()

        @pl.loop(0, per)
        def _(q, k=k):
            p = back_order.index(k) * per + q
            i = ((rep + k) % n_rep) * per + q
            total = jnp.zeros((feats.shape[1], TILE), F32)
            for s in range(0, n_slot, GROUP):
                some = [feats[table_s[0, p * n_slot + s + t]] for t in range(GROUP)]
                total += dot(join(some), join([tiles[i, s + t] for t in range(GROUP)]), NT)
            agg_mine[k, q] = total.astype(BF16)

        if k:
            c = send(agg_mine.at[k], agg.at[rep], ss_agg.at[k - 1], rs_agg.at[k - 1], rep_at(k))
            c.start()
            agg_sends.append(c)
    agg[rep] = agg_mine[0]

    for c in pre_sends:
        c.wait_recv()
    load_c.wait()
    n_hid = weights.shape[1]
    for j in range(n_rep):
        weight_fh[:, j * n_hid:(j + 1) * n_hid] = weights[j].astype(F32).T.astype(BF16)
        bias_col[j] = jnp.broadcast_to(biases[j, 0:1, :], (TILE, TILE)).T[0:n_hid, :]

    for c in agg_sends:
        c.wait_recv()

    width = agg.shape[2]
    whole = jnp.concatenate([agg[:, q].reshape(n_rep * width, TILE) for q in range(per)], axis=1)
    hid_sends = []
    for j in range(n_rep):
        wide_bias = jnp.concatenate([bias_col[j]] * (span // TILE), axis=1)
        pre = dot(weights[j], whole, NN) + wide_bias
        sigma = jax.nn.sigmoid(pre)
        hid_mine[j] = (pre * sigma).astype(BF16)
        delta[j] = (cots[j].astype(F32) * sigma * (1.0 + pre * (1.0 - sigma))).astype(BF16)
    deltas = delta[...].reshape(n_rep * n_hid, span)
    back_full = dot(weight_fh[...], deltas, NN).astype(BF16)
    for q in range(per):
        back_mine[:, q] = back_full[:, q * TILE:(q + 1) * TILE].reshape(n_rep, width, TILE)
    ones = jnp.ones((8, span), BF16)
    team_sends = []
    for j in range(n_rep):
        grad = dot(delta[j], whole, NT)
        bias_grad = jnp.pad(dot(ones, delta[j], NT)[0:1, :], ((0, 0), (0, TILE - n_hid)))
        for m in range(n_x):
            team_mine[j, m, 0:16, :] = grad[16 * m:16 * (m + 1), :]
            team_mine[j, m, 16:17, :] = bias_grad
    back_sends = []
    for k in range(1, n_rep):
        c = send(back_mine.at[(rep + k) % n_rep], back.at[rep], ss_back.at[k - 1], rs_back.at[k - 1], rep_at(k))
        c.start()
        back_sends.append(c)
    back[rep] = back_mine[rep]
    for n, (k, m) in enumerate(team):
        c = send(
            team_mine.at[(rep + k) % n_rep, (chip + m) % n_x, 0:17], team_in.at[rep, chip, 0:17],
            ss_team.at[n], rs_team.at[n], team_at(k, m),
        )
        c.start()
        team_sends.append(c)
    team_in[rep, chip, 0:17] = team_mine[rep, chip, 0:17]
    for n, k in enumerate(back_order):
        if k:
            back_sends[n_rep - k - 1].wait_recv()

        @pl.loop(0, per)
        def _(q, n=n, k=k):
            chunk = (rep + k) % n_rep
            lhs = back[chunk, q]
            for s in range(0, n_slot, BACK_GROUP):
                some = dot(lhs, join([tiles[chunk * per + q, s + t] for t in range(BACK_GROUP)]), NN)
                for u in range(BACK_GROUP):
                    t = (n * per + q) * n_slot + s + u
                    run[t] = some[:, u * TILE:(u + 1) * TILE] + run[table_s[1, t]]

    for c in team_sends:
        c.wait_recv()
    s3_mine[0:17, :] = sum(team_in[k, m, 0:17] for k in range(n_rep) for m in range(n_x))
    s3_sends = []
    for n, o in enumerate(column):
        c = send(s3_mine.at[0:17], s3_in.at[layer, core, 0:17], ss_s3.at[n], rs_s3.at[n], column_at(*o))
        c.start()
        s3_sends.append(c)
    part_sends = {}
    for g in feat_order:
        for b in range(n_blk):
            part[g, b] = run[table_s[2, g * n_blk + b]].astype(BF16)
        part_sends[g] = send(
            part.at[g], part_in.at[g], ss_part.at[g], rs_part.at[g], row_at(offsets[g])
        )
        part_sends[g].start()

    s3_in[layer, core, 0:17] = s3_mine[0:17, :]
    for k in range(1, n_rep):
        c = send(hid_mine.at[(rep + k) % n_rep], hid_out.at[:, mine], ss_hid.at[k - 1], rs_hid.at[k - 1], rep_at(k))
        c.start()
        hid_sends.append(c)
    keep_hid = pltpu.make_async_copy(hid_mine.at[rep], hid_out.at[:, mine], sem_local.at[3])
    keep_hid.start()

    for c in s3_sends:
        c.wait_recv()
    done = sum(s3_in[m, c, 0:17] for m in range(depth) for c in range(2))
    gw_mine[...] = done[0:16, :]
    gb_mine[...] = jnp.broadcast_to(done[16:17, :], gb_mine.shape)
    keep_gb = pltpu.make_async_copy(gb_mine, gb_out, sem_local.at[5])
    keep_gb.start()
    my_rows = pl.ds(pl.multiple_of(chip * 16, 16), 16)
    s4_sends = []
    for k in chips:
        c = send(gw_mine, gw_out.at[my_rows, :], ss_s4.at[k - 1], rs_s4.at[k - 1], team_at(0, k))
        c.start()
        s4_sends.append(c)
    keep_gw = pltpu.make_async_copy(gw_mine, gw_out.at[my_rows, :], sem_local.at[4])
    keep_gw.start()

    for g in far_first:
        part_sends[g].wait_recv()
    for b in range(n_blk):
        value = run[table_s[2, OWN * n_blk + b]]
        for g in far_first:
            value += part_in[g, b].astype(F32)
        gf_mine[:, b * TILE:(b + 1) * TILE] = value.astype(BF16)
    keep_gf = pltpu.make_async_copy(gf_mine, gf_out, sem_local.at[2])
    keep_gf.start()

    for c in hid_sends + s4_sends:
        c.wait_recv()
    keep_hid.wait()
    keep_gw.wait()
    keep_gb.wait()
    keep_gf.wait()
    everything = [feat_sends[g] for g in far_first] + pre_sends + agg_sends + back_sends + hid_sends
    everything += team_sends + s3_sends + s4_sends + [part_sends[g] for g in far_first]
    for c in everything:
        c.wait_send()


def finish(hid_in, gw_in, gb_in, gf_in, hid_out, gw_out, gb_out, gf_out, hid, gw, gb, gf, sems):
    through = ((hid_in, hid, hid_out), (gf_in, gf, gf_out), (gw_in, gw, gw_out))
    loads = [pltpu.make_async_copy(a, b, sems.at[0, n]) for n, (a, b, c) in enumerate(through)]
    loads.append(pltpu.make_async_copy(gb_in, gb, sems.at[0, 3]))
    stores = [pltpu.make_async_copy(b, c, sems.at[1, n]) for n, (a, b, c) in enumerate(through)]
    for c in loads:
        c.start()
    for n, c in enumerate(stores):
        loads[n].wait()
        c.start()
    loads[3].wait()
    gb_out[...] = gb[0:1, 0:gb_out.shape[1]]
    for c in stores:
        c.wait()


def body(n_row, n_rep, plane, features, tiles, tile_cols, counts, weight, bias, cotangent):
    n_blk, n_slot = tiles.shape[:2]
    rows, width = features.shape
    n_hid = weight.shape[1]
    fin = weight.shape[0]
    span = rows // n_rep
    depth = n_row // plane
    n_far = len(OFFSETS)
    n_slots = n_blk * n_slot
    dma = pltpu.SemaphoreType.DMA
    vmem = pl.BlockSpec(memory_space=pltpu.VMEM)
    smem = pl.BlockSpec(memory_space=pltpu.SMEM)
    hbm = pl.BlockSpec(memory_space=pltpu.HBM)

    def pair(*shape):
        return [dma(shape), dma(shape)]

    out = pl.pallas_call(
        functools.partial(kernel, n_row, n_rep, plane),
        out_shape=(
            jax.ShapeDtypeStruct((n_hid, rows), BF16),
            jax.ShapeDtypeStruct((n_hid, fin), F32),
            jax.ShapeDtypeStruct((8, TILE), F32),
            jax.ShapeDtypeStruct((width, rows), BF16),
        ),
        in_specs=[hbm] * 7,
        out_specs=(hbm, hbm, hbm, hbm),
        scratch_shapes=[
            pltpu.VMEM(tile_cols.shape, jnp.int32),
            pltpu.SMEM(counts.shape, jnp.int32),
            pltpu.VMEM((1, n_hid), F32),
            pltpu.VMEM(tiles.shape, BF16),
            pltpu.VMEM((len(OFFSETS) * n_blk + 1, width, TILE), BF16),
            pltpu.VMEM((n_rep, n_hid, span), BF16),
            pltpu.VMEM((n_rep, n_hid, fin), BF16),
            pltpu.VMEM((n_rep, 8, TILE), F32),
            pltpu.VMEM((fin, n_rep * n_hid), BF16),
            pltpu.VMEM((n_rep, n_hid, TILE), F32),
            pltpu.VMEM((n_blk, TILE), jnp.int32),
            pltpu.VMEM((8, TILE), jnp.int32),
            pltpu.SMEM((8, TILE), jnp.int32),
            pltpu.VMEM((n_rep, n_blk // n_rep, width, TILE), BF16),
            pltpu.VMEM((n_rep, n_blk // n_rep, width, TILE), BF16),
            pltpu.VMEM((n_rep, n_hid, span), BF16),
            pltpu.VMEM((n_rep, n_hid, span), BF16),
            pltpu.VMEM((n_rep, n_blk // n_rep, width, TILE), BF16),
            pltpu.VMEM((n_rep, n_blk // n_rep, width, TILE), BF16),
            pltpu.VMEM((n_slots + 1, width, TILE), F32),
            pltpu.VMEM((n_far, n_blk, width, TILE), BF16),
            pltpu.VMEM((n_far, n_blk, width, TILE), BF16),
            pltpu.VMEM((n_rep, plane // 2, 24, TILE), F32),
            pltpu.VMEM((n_rep, plane // 2, 24, TILE), F32),
            pltpu.VMEM((24, TILE), F32),
            pltpu.VMEM((depth, 2, 24, TILE), F32),
            pltpu.VMEM((16, TILE), F32),
            pltpu.VMEM((8, TILE), F32),
            pltpu.VMEM((width, rows), BF16),
            dma((n_blk,)),
            dma((n_rep,)),
            dma((8,)),
            *pair(n_far),
            *pair(3, n_rep - 1),
            *pair(n_rep - 1),
            *pair(n_rep - 1),
            *pair(n_rep - 1),
            *pair(n_rep * plane // 2 - 1),
            *pair(depth * 2 - 1),
            *pair(plane // 2 - 1),
            *pair(n_far),
        ],
        compiler_params=pltpu.CompilerParams(
            collective_id=0, has_side_effects=True, vmem_limit_bytes=62 * 1024 * 1024
        ),
        cost_estimate=pl.CostEstimate(
            flops=4 * n_slots * TILE * TILE * width, bytes_accessed=tiles.size * 2, transcendentals=span * n_rep * n_hid
        ),
    )(
        tile_cols, counts, bias.reshape(1, n_hid), features.T, tiles, weight.T, cotangent.T,
    )
    hidden, grad_weight, grad_bias, grad_features = pl.pallas_call(
        finish,
        out_shape=(
            jax.ShapeDtypeStruct((n_hid, rows), BF16),
            jax.ShapeDtypeStruct((n_hid, fin), F32),
            jax.ShapeDtypeStruct((1, n_hid), F32),
            jax.ShapeDtypeStruct((width, rows), BF16),
        ),
        in_specs=[hbm] * 4,
        out_specs=(hbm, hbm, vmem, hbm),
        scratch_shapes=[
            pltpu.VMEM((n_hid, rows), BF16),
            pltpu.VMEM((n_hid, fin), F32),
            pltpu.VMEM((8, TILE), F32),
            pltpu.VMEM((width, rows), BF16),
            dma((2, 4)),
        ],
        compiler_params=pltpu.CompilerParams(vmem_limit_bytes=62 * 1024 * 1024),
    )(*out)
    return hidden.T, grad_weight.T, grad_bias.reshape(n_hid), grad_features.T


def solution(mesh):
    in_specs = (
        P("row", "rep"),
        P("row", None, None, None),
        P("row", None),
        P("row"),
        P(None, "rep"),
        P("rep"),
        P("row", "rep"),
    )
    out_specs = (P("row", "rep"), P(None, "rep"), P("rep"), P("row", "rep"))
    n_row, n_rep = mesh.shape["row"], mesh.shape["rep"]
    step = functools.partial(body, n_row, n_rep, 8)
    return jax.shard_map(step, mesh=mesh, in_specs=in_specs, out_specs=out_specs, check_vma=False)
```

```python
import functools

import jax
import jax.numpy as jnp
from jax import lax
from jax.experimental import pallas as pl
from jax.experimental.pallas import tpu as pltpu
from jax.sharding import PartitionSpec as P

F32 = jnp.float32
BF16 = jnp.bfloat16
TILE = 128
OFFSETS = (-2, -1, 0, 1, 2, None)
OWN = 2
FAR = 5
GROUP = 2
BACK_GROUP = 2
NT = (((1,), (1,)), ((), ()))
NN = (((1,), (0,)), ((), ()))


def dot(a, b, dims):
    return lax.dot_general(a, b, dims, preferred_element_type=F32)


def join(parts):
    return jnp.concatenate(parts, axis=1) if len(parts) > 1 else parts[0]


def kernel(
    n_row, n_rep, plane,
    cols_hbm, counts_hbm, bias_hbm, ft_ref, tiles_ref, wt_ref, ct_ref,
    hid_out, gw_out, gb_out, gf_out,
    cols_ref, counts_ref, bias_ref, tiles, feats, cots, weights, biases, weight_fh, bias_col, keys_2d, table, table_s,
    agg_mine, agg, hid_mine, delta, back_mine, back, run, part, part_in,
    team_mine, team_in, s3_mine, s3_in, gw_mine, gb_mine, gf_mine,
    sem_feat, sem_tile, sem_local,
    ss_feat, rs_feat, ss_pre, rs_pre, ss_agg, rs_agg, ss_back, rs_back, ss_hid, rs_hid,
    ss_team, rs_team, ss_s3, rs_s3, ss_s4, rs_s4, ss_part, rs_part,
):
    row = lax.axis_index("row")
    rep = lax.axis_index("rep")
    depth = n_row // plane
    layer = row // plane
    spot = row % plane
    n_blk = tiles_ref.shape[0]
    n_slot = tiles_ref.shape[1]
    per = n_blk // n_rep
    span = per * TILE
    none_feat = len(OFFSETS) * n_blk
    n_slots = n_blk * n_slot
    offsets = [n_row // 2 if o is None else o for o in OFFSETS]
    far_first = (5, 0, 4, 1, 3)
    feat_order = (0, 4, 5, 1, 3)
    hops = [min(k, n_rep - k) for k in range(n_rep)]
    near_last = sorted(range(1, n_rep), key=lambda k: -hops[k])
    order = near_last + [0]
    n_x = plane // 2
    chip = spot // 2
    core = spot % 2
    team = [(k, m) for k in range(n_rep) for m in range(n_x) if (k, m) != (0, 0)]
    team.sort(key=lambda o: -hops[o[0]] - min(o[1], n_x - o[1]))
    column = [(k, c) for k in range(depth) for c in range(2) if (k, c) != (0, 0)]
    column.sort(key=lambda o: -min(o[0], depth - o[0]))
    chips = sorted(range(1, n_x), key=lambda m: -min(m, n_x - m))
    back_order = [0] + near_last[::-1]

    def block_at(p, q=0):
        return ((rep + back_order[p // per]) % n_rep) * per + p % per + q

    def row_at(offset):
        return {"row": (row + offset + n_row) % n_row, "rep": rep}

    def rep_at(k):
        return {"row": row, "rep": (rep + k) % n_rep}

    def team_at(k, m):
        return {"row": layer * plane + (chip + m) % n_x * 2 + core, "rep": (rep + k) % n_rep}

    def column_at(k, c):
        return {"row": (layer + k) % depth * plane + chip * 2 + (core + c) % 2, "rep": rep}

    def send(src, dst, ss, rs, where):
        return pltpu.make_async_remote_copy(
            src_ref=src, dst_ref=dst, send_sem=ss, recv_sem=rs,
            device_id=where, device_id_type=pl.DeviceIdType.MESH,
        )

    barrier = pltpu.get_barrier_semaphore()
    peers = [row_at(offsets[g]) for g in far_first]
    peers += [team_at(*o) for o in team]
    peers += [column_at(*o) for o in column]
    for where in peers:
        pl.semaphore_signal(barrier, inc=1, device_id=where, device_id_type=pl.DeviceIdType.MESH)

    feat_loads = [
        pltpu.make_async_copy(ft_ref.at[:, TILE * b:TILE * (b + 1)], feats.at[OWN * n_blk + b], sem_feat.at[b])
        for b in range(n_blk)
    ]
    for c in feat_loads:
        c.start()
    mine = pl.ds(pl.multiple_of(rep * span, span), span)
    load_w = pltpu.make_async_copy(wt_ref, weights.at[rep], sem_local.at[0])
    load_c = pltpu.make_async_copy(ct_ref.at[:, mine], cots.at[rep], sem_local.at[1])
    load_cols = pltpu.make_async_copy(cols_hbm, cols_ref, sem_local.at[5])
    load_counts = pltpu.make_async_copy(counts_hbm, counts_ref, sem_local.at[6])
    load_bias = pltpu.make_async_copy(bias_hbm, bias_ref, sem_local.at[7])
    for c in (load_w, load_bias, load_cols, load_counts, load_c):
        c.start()
    tile_loads = []
    for k in range(n_rep):
        which = pl.ds(((rep + k) % n_rep) * per, per)
        tile_loads.append(
            pltpu.make_async_copy(tiles_ref.at[which], tiles.at[which], sem_tile.at[k])
        )
    for k in order:
        tile_loads[k].start()

    pl.semaphore_wait(barrier, len(peers))

    for c in feat_loads:
        c.wait()
    feat_sends = {
        g: send(
            feats.at[OWN * n_blk:(OWN + 1) * n_blk], feats.at[g * n_blk:(g + 1) * n_blk],
            ss_feat.at[g], rs_feat.at[g], row_at(-offsets[g]),
        )
        for g in far_first
    }
    for g in feat_order:
        feat_sends[g].start()
    load_w.wait()
    load_bias.wait()
    biases[rep] = jnp.broadcast_to(jnp.pad(bias_ref[...], ((0, 0), (0, TILE - bias_ref.shape[1]))), (8, TILE))
    pre_sends = []
    for k in range(1, n_rep):
        pre_sends.append(send(weights.at[rep], weights.at[rep], ss_pre.at[0, k - 1], rs_pre.at[0, k - 1], rep_at(k)))
        pre_sends.append(send(biases.at[rep], biases.at[rep], ss_pre.at[1, k - 1], rs_pre.at[1, k - 1], rep_at(k)))
        pre_sends.append(
            send(
                ct_ref.at[:, pl.ds(pl.multiple_of(((rep + k) % n_rep) * span, span), span)],
                cots.at[rep], ss_pre.at[2, k - 1], rs_pre.at[2, k - 1], rep_at(k),
            )
        )
    for c in pre_sends:
        c.start()

    load_cols.wait()
    load_counts.wait()
    cols = cols_ref[...]
    shape = cols.shape
    slot = lax.broadcasted_iota(jnp.int32, shape, 1)
    line = lax.broadcasted_iota(jnp.int32, shape, 0)
    count = jnp.zeros(shape, jnp.int32)
    for i in range(n_blk):
        count = jnp.where(line == i, counts_ref[i], count)
    group = jnp.minimum((cols // n_blk - row + 2 + n_row) % n_row, 5)
    key = jnp.where(slot < count, group * n_blk + cols % n_blk, none_feat)
    keys_2d[:, 0:n_slot] = key
    keys = jnp.concatenate([keys_2d[pl.ds(block_at(p), 1), 0:n_slot] for p in range(n_blk)], axis=1)
    by_lane = jnp.broadcast_to(keys, (n_slots, n_slots))
    by_line = by_lane.T
    up = lax.broadcasted_iota(jnp.int32, (n_slots, n_slots), 0)
    across = lax.broadcasted_iota(jnp.int32, (n_slots, n_slots), 1)
    before = jnp.max(jnp.where((by_line == by_lane) & (up < across), up, -1), axis=0, keepdims=True)
    last = jnp.max(jnp.where(by_line == across, up, -1), axis=0, keepdims=True)
    table[0:1, :] = keys
    table[1:2, :] = jnp.where(before < 0, n_slots, before)
    table[2:3, :] = jnp.where(last < 0, n_slots, last)
    table[3:8, :] = jnp.zeros((5, n_slots), jnp.int32)
    to_scalar = pltpu.make_async_copy(table, table_s, sem_local.at[2])
    to_scalar.start()
    feats[none_feat] = jnp.zeros(feats.shape[1:], BF16)
    run[n_slots] = jnp.zeros(run.shape[1:], F32)
    to_scalar.wait()

    for g in far_first:
        feat_sends[g].wait_recv()

    agg_sends = []
    for k in order:
        tile_loads[k].wait()

        @pl.loop(0, per, unroll=True)
        def _(q, k=k):
            p = back_order.index(k) * per + q
            i = ((rep + k) % n_rep) * per + q
            total = jnp.zeros((feats.shape[1], TILE), F32)
            for s in range(0, n_slot, GROUP):
                some = [feats[table_s[0, p * n_slot + s + t]] for t in range(GROUP)]
                total += dot(join(some), join([tiles[i, s + t] for t in range(GROUP)]), NT)
            agg_mine[k, q] = total.astype(BF16)

        if k:
            c = send(agg_mine.at[k], agg.at[rep], ss_agg.at[k - 1], rs_agg.at[k - 1], rep_at(k))
            c.start()
            agg_sends.append(c)
    agg[rep] = agg_mine[0]

    for c in pre_sends:
        c.wait_recv()
    load_c.wait()
    n_hid = weights.shape[1]
    for j in range(n_rep):
        weight_fh[:, j * n_hid:(j + 1) * n_hid] = weights[j].astype(F32).T.astype(BF16)
        bias_col[j] = jnp.broadcast_to(biases[j, 0:1, :], (TILE, TILE)).T[0:n_hid, :]

    for c in agg_sends:
        c.wait_recv()

    width = agg.shape[2]
    whole = jnp.concatenate([agg[:, q].reshape(n_rep * width, TILE) for q in range(per)], axis=1)
    hid_sends = []
    for j in range(n_rep):
        wide_bias = jnp.concatenate([bias_col[j]] * (span // TILE), axis=1)
        pre = dot(weights[j], whole, NN) + wide_bias
        sigma = jax.nn.sigmoid(pre)
        hid_mine[j] = (pre * sigma).astype(BF16)
        delta[j] = (cots[j].astype(F32) * sigma * (1.0 + pre * (1.0 - sigma))).astype(BF16)
    deltas = delta[...].reshape(n_rep * n_hid, span)
    back_full = dot(weight_fh[...], deltas, NN).astype(BF16)
    for q in range(per):
        back_mine[:, q] = back_full[:, q * TILE:(q + 1) * TILE].reshape(n_rep, width, TILE)
    ones = jnp.ones((8, span), BF16)
    team_sends = []
    for j in range(n_rep):
        grad = dot(delta[j], whole, NT)
        bias_grad = jnp.pad(dot(ones, delta[j], NT)[0:1, :], ((0, 0), (0, TILE - n_hid)))
        for m in range(n_x):
            team_mine[j, m, 0:16, :] = grad[16 * m:16 * (m + 1), :]
            team_mine[j, m, 16:17, :] = bias_grad
    back_sends = []
    for k in range(1, n_rep):
        c = send(back_mine.at[(rep + k) % n_rep], back.at[rep], ss_back.at[k - 1], rs_back.at[k - 1], rep_at(k))
        c.start()
        back_sends.append(c)
    back[rep] = back_mine[rep]
    for n, (k, m) in enumerate(team):
        c = send(
            team_mine.at[(rep + k) % n_rep, (chip + m) % n_x, 0:17], team_in.at[rep, chip, 0:17],
            ss_team.at[n], rs_team.at[n], team_at(k, m),
        )
        c.start()
        team_sends.append(c)
    team_in[rep, chip, 0:17] = team_mine[rep, chip, 0:17]
    for n, k in enumerate(back_order):
        if k:
            back_sends[n_rep - k - 1].wait_recv()

        @pl.loop(0, per, unroll=True)
        def _(q, n=n, k=k):
            chunk = (rep + k) % n_rep
            lhs = back[chunk, q]
            for s in range(0, n_slot, BACK_GROUP):
                some = dot(lhs, join([tiles[chunk * per + q, s + t] for t in range(BACK_GROUP)]), NN)
                for u in range(BACK_GROUP):
                    t = (n * per + q) * n_slot + s + u
                    run[t] = some[:, u * TILE:(u + 1) * TILE] + run[table_s[1, t]]

    for c in team_sends:
        c.wait_recv()
    s3_mine[0:17, :] = sum(team_in[k, m, 0:17] for k in range(n_rep) for m in range(n_x))
    s3_sends = []
    for n, o in enumerate(column):
        c = send(s3_mine.at[0:17], s3_in.at[layer, core, 0:17], ss_s3.at[n], rs_s3.at[n], column_at(*o))
        c.start()
        s3_sends.append(c)
    part_sends = {}
    for g in feat_order:
        for b in range(n_blk):
            part[g, b] = run[table_s[2, g * n_blk + b]].astype(BF16)
        part_sends[g] = send(
            part.at[g], part_in.at[g], ss_part.at[g], rs_part.at[g], row_at(offsets[g])
        )
        part_sends[g].start()

    s3_in[layer, core, 0:17] = s3_mine[0:17, :]
    for k in range(1, n_rep):
        c = send(hid_mine.at[(rep + k) % n_rep], hid_out.at[:, mine], ss_hid.at[k - 1], rs_hid.at[k - 1], rep_at(k))
        c.start()
        hid_sends.append(c)
    keep_hid = pltpu.make_async_copy(hid_mine.at[rep], hid_out.at[:, mine], sem_local.at[3])
    keep_hid.start()

    for c in s3_sends:
        c.wait_recv()
    done = sum(s3_in[m, c, 0:17] for m in range(depth) for c in range(2))
    gw_mine[...] = done[0:16, :]
    gb_mine[...] = jnp.broadcast_to(done[16:17, :], gb_mine.shape)
    keep_gb = pltpu.make_async_copy(gb_mine, gb_out, sem_local.at[5])
    keep_gb.start()
    my_rows = pl.ds(pl.multiple_of(chip * 16, 16), 16)
    s4_sends = []
    for k in chips:
        c = send(gw_mine, gw_out.at[my_rows, :], ss_s4.at[k - 1], rs_s4.at[k - 1], team_at(0, k))
        c.start()
        s4_sends.append(c)
    keep_gw = pltpu.make_async_copy(gw_mine, gw_out.at[my_rows, :], sem_local.at[4])
    keep_gw.start()

    for g in far_first:
        part_sends[g].wait_recv()
    for b in range(n_blk):
        value = run[table_s[2, OWN * n_blk + b]]
        for g in far_first:
            value += part_in[g, b].astype(F32)
        gf_mine[:, b * TILE:(b + 1) * TILE] = value.astype(BF16)
    keep_gf = pltpu.make_async_copy(gf_mine, gf_out, sem_local.at[2])
    keep_gf.start()

    for c in hid_sends + s4_sends:
        c.wait_recv()
    keep_hid.wait()
    keep_gw.wait()
    keep_gb.wait()
    keep_gf.wait()
    everything = [feat_sends[g] for g in far_first] + pre_sends + agg_sends + back_sends + hid_sends
    everything += team_sends + s3_sends + s4_sends + [part_sends[g] for g in far_first]
    for c in everything:
        c.wait_send()


def finish(hid_in, gw_in, gb_in, gf_in, hid_out, gw_out, gb_out, gf_out, hid, gw, gb, gf, sems):
    through = ((hid_in, hid, hid_out), (gf_in, gf, gf_out), (gw_in, gw, gw_out))
    loads = [pltpu.make_async_copy(a, b, sems.at[0, n]) for n, (a, b, c) in enumerate(through)]
    loads.append(pltpu.make_async_copy(gb_in, gb, sems.at[0, 3]))
    stores = [pltpu.make_async_copy(b, c, sems.at[1, n]) for n, (a, b, c) in enumerate(through)]
    for c in loads:
        c.start()
    for n, c in enumerate(stores):
        loads[n].wait()
        c.start()
    loads[3].wait()
    gb_out[...] = gb[0:1, 0:gb_out.shape[1]]
    for c in stores:
        c.wait()


def body(n_row, n_rep, plane, features, tiles, tile_cols, counts, weight, bias, cotangent):
    n_blk, n_slot = tiles.shape[:2]
    rows, width = features.shape
    n_hid = weight.shape[1]
    fin = weight.shape[0]
    span = rows // n_rep
    depth = n_row // plane
    n_far = len(OFFSETS)
    n_slots = n_blk * n_slot
    dma = pltpu.SemaphoreType.DMA
    vmem = pl.BlockSpec(memory_space=pltpu.VMEM)
    smem = pl.BlockSpec(memory_space=pltpu.SMEM)
    hbm = pl.BlockSpec(memory_space=pltpu.HBM)

    def pair(*shape):
        return [dma(shape), dma(shape)]

    out = pl.pallas_call(
        functools.partial(kernel, n_row, n_rep, plane),
        out_shape=(
            jax.ShapeDtypeStruct((n_hid, rows), BF16),
            jax.ShapeDtypeStruct((n_hid, fin), F32),
            jax.ShapeDtypeStruct((8, TILE), F32),
            jax.ShapeDtypeStruct((width, rows), BF16),
        ),
        in_specs=[hbm] * 7,
        out_specs=(hbm, hbm, hbm, hbm),
        scratch_shapes=[
            pltpu.VMEM(tile_cols.shape, jnp.int32),
            pltpu.SMEM(counts.shape, jnp.int32),
            pltpu.VMEM((1, n_hid), F32),
            pltpu.VMEM(tiles.shape, BF16),
            pltpu.VMEM((len(OFFSETS) * n_blk + 1, width, TILE), BF16),
            pltpu.VMEM((n_rep, n_hid, span), BF16),
            pltpu.VMEM((n_rep, n_hid, fin), BF16),
            pltpu.VMEM((n_rep, 8, TILE), F32),
            pltpu.VMEM((fin, n_rep * n_hid), BF16),
            pltpu.VMEM((n_rep, n_hid, TILE), F32),
            pltpu.VMEM((n_blk, TILE), jnp.int32),
            pltpu.VMEM((8, TILE), jnp.int32),
            pltpu.SMEM((8, TILE), jnp.int32),
            pltpu.VMEM((n_rep, n_blk // n_rep, width, TILE), BF16),
            pltpu.VMEM((n_rep, n_blk // n_rep, width, TILE), BF16),
            pltpu.VMEM((n_rep, n_hid, span), BF16),
            pltpu.VMEM((n_rep, n_hid, span), BF16),
            pltpu.VMEM((n_rep, n_blk // n_rep, width, TILE), BF16),
            pltpu.VMEM((n_rep, n_blk // n_rep, width, TILE), BF16),
            pltpu.VMEM((n_slots + 1, width, TILE), F32),
            pltpu.VMEM((n_far, n_blk, width, TILE), BF16),
            pltpu.VMEM((n_far, n_blk, width, TILE), BF16),
            pltpu.VMEM((n_rep, plane // 2, 24, TILE), F32),
            pltpu.VMEM((n_rep, plane // 2, 24, TILE), F32),
            pltpu.VMEM((24, TILE), F32),
            pltpu.VMEM((depth, 2, 24, TILE), F32),
            pltpu.VMEM((16, TILE), F32),
            pltpu.VMEM((8, TILE), F32),
            pltpu.VMEM((width, rows), BF16),
            dma((n_blk,)),
            dma((n_rep,)),
            dma((8,)),
            *pair(n_far),
            *pair(3, n_rep - 1),
            *pair(n_rep - 1),
            *pair(n_rep - 1),
            *pair(n_rep - 1),
            *pair(n_rep * plane // 2 - 1),
            *pair(depth * 2 - 1),
            *pair(plane // 2 - 1),
            *pair(n_far),
        ],
        compiler_params=pltpu.CompilerParams(
            collective_id=0, has_side_effects=True, vmem_limit_bytes=62 * 1024 * 1024
        ),
        cost_estimate=pl.CostEstimate(
            flops=4 * n_slots * TILE * TILE * width, bytes_accessed=tiles.size * 2, transcendentals=span * n_rep * n_hid
        ),
    )(
        tile_cols, counts, bias.reshape(1, n_hid), features.T, tiles, weight.T, cotangent.T,
    )
    hidden, grad_weight, grad_bias, grad_features = pl.pallas_call(
        finish,
        out_shape=(
            jax.ShapeDtypeStruct((n_hid, rows), BF16),
            jax.ShapeDtypeStruct((n_hid, fin), F32),
            jax.ShapeDtypeStruct((1, n_hid), F32),
            jax.ShapeDtypeStruct((width, rows), BF16),
        ),
        in_specs=[hbm] * 4,
        out_specs=(hbm, hbm, vmem, hbm),
        scratch_shapes=[
            pltpu.VMEM((n_hid, rows), BF16),
            pltpu.VMEM((n_hid, fin), F32),
            pltpu.VMEM((8, TILE), F32),
            pltpu.VMEM((width, rows), BF16),
            dma((2, 4)),
        ],
        compiler_params=pltpu.CompilerParams(vmem_limit_bytes=62 * 1024 * 1024),
    )(*out)
    return hidden.T, grad_weight.T, grad_bias.reshape(n_hid), grad_features.T


def solution(mesh):
    in_specs = (
        P("row", "rep"),
        P("row", None, None, None),
        P("row", None),
        P("row"),
        P(None, "rep"),
        P("rep"),
        P("row", "rep"),
    )
    out_specs = (P("row", "rep"), P(None, "rep"), P("rep"), P("row", "rep"))
    n_row, n_rep = mesh.shape["row"], mesh.shape["rep"]
    step = functools.partial(body, n_row, n_rep, 8)
    return jax.shard_map(step, mesh=mesh, in_specs=in_specs, out_specs=out_specs, check_vma=False)
```

```python
import functools

import jax
import jax.numpy as jnp
from jax import lax
from jax.experimental import pallas as pl
from jax.experimental.pallas import tpu as pltpu
from jax.sharding import PartitionSpec as P

F32 = jnp.float32
BF16 = jnp.bfloat16
TILE = 128
OFFSETS = (-2, -1, 0, 1, 2, None)
OWN = 2
FAR = 5
GROUP = 4
BACK_GROUP = 4
NT = (((1,), (1,)), ((), ()))
NN = (((1,), (0,)), ((), ()))


def dot(a, b, dims):
    return lax.dot_general(a, b, dims, preferred_element_type=F32)


def join(parts):
    return jnp.concatenate(parts, axis=1) if len(parts) > 1 else parts[0]


def kernel(
    n_row, n_rep, plane,
    cols_hbm, counts_hbm, bias_hbm, ft_ref, tiles_ref, wt_ref, ct_ref,
    hid_out, gw_out, gb_out, gf_out,
    cols_ref, counts_ref, bias_ref, tiles, feats, cots, weights, biases, weight_fh, bias_col, keys_2d, table, table_s,
    agg_mine, agg, hid_mine, delta, back_mine, back, run, part, part_in,
    team_mine, team_in, s3_mine, s3_in, gw_mine, gb_mine, gf_mine,
    sem_feat, sem_tile, sem_local,
    ss_feat, rs_feat, ss_pre, rs_pre, ss_agg, rs_agg, ss_back, rs_back, ss_hid, rs_hid,
    ss_team, rs_team, ss_s3, rs_s3, ss_s4, rs_s4, ss_part, rs_part,
):
    row = lax.axis_index("row")
    rep = lax.axis_index("rep")
    depth = n_row // plane
    layer = row // plane
    spot = row % plane
    n_blk = tiles_ref.shape[0]
    n_slot = tiles_ref.shape[1]
    per = n_blk // n_rep
    span = per * TILE
    none_feat = len(OFFSETS) * n_blk
    n_slots = n_blk * n_slot
    offsets = [n_row // 2 if o is None else o for o in OFFSETS]
    far_first = (5, 0, 4, 1, 3)
    feat_order = (0, 4, 5, 1, 3)
    hops = [min(k, n_rep - k) for k in range(n_rep)]
    near_last = sorted(range(1, n_rep), key=lambda k: -hops[k])
    order = near_last + [0]
    n_x = plane // 2
    chip = spot // 2
    core = spot % 2
    team = [(k, m) for k in range(n_rep) for m in range(n_x) if (k, m) != (0, 0)]
    team.sort(key=lambda o: -hops[o[0]] - min(o[1], n_x - o[1]))
    column = [(k, c) for k in range(depth) for c in range(2) if (k, c) != (0, 0)]
    column.sort(key=lambda o: -min(o[0], depth - o[0]))
    chips = sorted(range(1, n_x), key=lambda m: -min(m, n_x - m))
    back_order = [0] + near_last[::-1]

    def block_at(p, q=0):
        return ((rep + back_order[p // per]) % n_rep) * per + p % per + q

    def row_at(offset):
        return {"row": (row + offset + n_row) % n_row, "rep": rep}

    def rep_at(k):
        return {"row": row, "rep": (rep + k) % n_rep}

    def team_at(k, m):
        return {"row": layer * plane + (chip + m) % n_x * 2 + core, "rep": (rep + k) % n_rep}

    def column_at(k, c):
        return {"row": (layer + k) % depth * plane + chip * 2 + (core + c) % 2, "rep": rep}

    def send(src, dst, ss, rs, where):
        return pltpu.make_async_remote_copy(
            src_ref=src, dst_ref=dst, send_sem=ss, recv_sem=rs,
            device_id=where, device_id_type=pl.DeviceIdType.MESH,
        )

    barrier = pltpu.get_barrier_semaphore()
    peers = [row_at(offsets[g]) for g in far_first]
    peers += [team_at(*o) for o in team]
    peers += [column_at(*o) for o in column]
    for where in peers:
        pl.semaphore_signal(barrier, inc=1, device_id=where, device_id_type=pl.DeviceIdType.MESH)

    feat_loads = [
        pltpu.make_async_copy(ft_ref.at[:, TILE * b:TILE * (b + 1)], feats.at[OWN * n_blk + b], sem_feat.at[b])
        for b in range(n_blk)
    ]
    for c in feat_loads:
        c.start()
    mine = pl.ds(pl.multiple_of(rep * span, span), span)
    load_w = pltpu.make_async_copy(wt_ref, weights.at[rep], sem_local.at[0])
    load_c = pltpu.make_async_copy(ct_ref.at[:, mine], cots.at[rep], sem_local.at[1])
    load_cols = pltpu.make_async_copy(cols_hbm, cols_ref, sem_local.at[5])
    load_counts = pltpu.make_async_copy(counts_hbm, counts_ref, sem_local.at[6])
    load_bias = pltpu.make_async_copy(bias_hbm, bias_ref, sem_local.at[7])
    for c in (load_w, load_bias, load_cols, load_counts, load_c):
        c.start()
    tile_loads = []
    for k in range(n_rep):
        which = pl.ds(((rep + k) % n_rep) * per, per)
        tile_loads.append(
            pltpu.make_async_copy(tiles_ref.at[which], tiles.at[which], sem_tile.at[k])
        )
    for k in order:
        tile_loads[k].start()

    pl.semaphore_wait(barrier, len(peers))

    for c in feat_loads:
        c.wait()
    feat_sends = {
        g: send(
            feats.at[OWN * n_blk:(OWN + 1) * n_blk], feats.at[g * n_blk:(g + 1) * n_blk],
            ss_feat.at[g], rs_feat.at[g], row_at(-offsets[g]),
        )
        for g in far_first
    }
    for g in feat_order:
        feat_sends[g].start()
    load_w.wait()
    load_bias.wait()
    biases[rep] = jnp.broadcast_to(jnp.pad(bias_ref[...], ((0, 0), (0, TILE - bias_ref.shape[1]))), (8, TILE))
    pre_sends = []
    for k in range(1, n_rep):
        pre_sends.append(send(weights.at[rep], weights.at[rep], ss_pre.at[0, k - 1], rs_pre.at[0, k - 1], rep_at(k)))
        pre_sends.append(send(biases.at[rep], biases.at[rep], ss_pre.at[1, k - 1], rs_pre.at[1, k - 1], rep_at(k)))
        pre_sends.append(
            send(
                ct_ref.at[:, pl.ds(pl.multiple_of(((rep + k) % n_rep) * span, span), span)],
                cots.at[rep], ss_pre.at[2, k - 1], rs_pre.at[2, k - 1], rep_at(k),
            )
        )
    for c in pre_sends:
        c.start()

    load_cols.wait()
    load_counts.wait()
    cols = cols_ref[...]
    shape = cols.shape
    slot = lax.broadcasted_iota(jnp.int32, shape, 1)
    line = lax.broadcasted_iota(jnp.int32, shape, 0)
    count = jnp.zeros(shape, jnp.int32)
    for i in range(n_blk):
        count = jnp.where(line == i, counts_ref[i], count)
    group = jnp.minimum((cols // n_blk - row + 2 + n_row) % n_row, 5)
    key = jnp.where(slot < count, group * n_blk + cols % n_blk, none_feat)
    keys_2d[:, 0:n_slot] = key
    keys = jnp.concatenate([keys_2d[pl.ds(block_at(p), 1), 0:n_slot] for p in range(n_blk)], axis=1)
    by_lane = jnp.broadcast_to(keys, (n_slots, n_slots))
    by_line = by_lane.T
    up = lax.broadcasted_iota(jnp.int32, (n_slots, n_slots), 0)
    across = lax.broadcasted_iota(jnp.int32, (n_slots, n_slots), 1)
    before = jnp.max(jnp.where((by_line == by_lane) & (up < across), up, -1), axis=0, keepdims=True)
    last = jnp.max(jnp.where(by_line == across, up, -1), axis=0, keepdims=True)
    table[0:1, :] = keys
    table[1:2, :] = jnp.where(before < 0, n_slots, before)
    table[2:3, :] = jnp.where(last < 0, n_slots, last)
    table[3:8, :] = jnp.zeros((5, n_slots), jnp.int32)
    to_scalar = pltpu.make_async_copy(table, table_s, sem_local.at[2])
    to_scalar.start()
    feats[none_feat] = jnp.zeros(feats.shape[1:], BF16)
    run[n_slots] = jnp.zeros(run.shape[1:], F32)
    to_scalar.wait()

    for g in far_first:
        feat_sends[g].wait_recv()

    agg_sends = []
    for k in order:
        tile_loads[k].wait()

        @pl.loop(0, per, unroll=True)
        def _(q, k=k):
            p = back_order.index(k) * per + q
            i = ((rep + k) % n_rep) * per + q
            total = jnp.zeros((feats.shape[1], TILE), F32)
            for s in range(0, n_slot, GROUP):
                some = [feats[table_s[0, p * n_slot + s + t]] for t in range(GROUP)]
                total += dot(join(some), join([tiles[i, s + t] for t in range(GROUP)]), NT)
            agg_mine[k, q] = total.astype(BF16)

        if k:
            c = send(agg_mine.at[k], agg.at[rep], ss_agg.at[k - 1], rs_agg.at[k - 1], rep_at(k))
            c.start()
            agg_sends.append(c)
    agg[rep] = agg_mine[0]

    for c in pre_sends:
        c.wait_recv()
    load_c.wait()
    n_hid = weights.shape[1]
    for j in range(n_rep):
        weight_fh[:, j * n_hid:(j + 1) * n_hid] = weights[j].astype(F32).T.astype(BF16)
        bias_col[j] = jnp.broadcast_to(biases[j, 0:1, :], (TILE, TILE)).T[0:n_hid, :]

    for c in agg_sends:
        c.wait_recv()

    width = agg.shape[2]
    whole = jnp.concatenate([agg[:, q].reshape(n_rep * width, TILE) for q in range(per)], axis=1)
    hid_sends = []
    for j in range(n_rep):
        wide_bias = jnp.concatenate([bias_col[j]] * (span // TILE), axis=1)
        pre = dot(weights[j], whole, NN) + wide_bias
        sigma = jax.nn.sigmoid(pre)
        hid_mine[j] = (pre * sigma).astype(BF16)
        delta[j] = (cots[j].astype(F32) * sigma * (1.0 + pre * (1.0 - sigma))).astype(BF16)
    deltas = delta[...].reshape(n_rep * n_hid, span)
    back_full = dot(weight_fh[...], deltas, NN).astype(BF16)
    for q in range(per):
        back_mine[:, q] = back_full[:, q * TILE:(q + 1) * TILE].reshape(n_rep, width, TILE)
    ones = jnp.ones((8, span), BF16)
    team_sends = []
    for j in range(n_rep):
        grad = dot(delta[j], whole, NT)
        bias_grad = jnp.pad(dot(ones, delta[j], NT)[0:1, :], ((0, 0), (0, TILE - n_hid)))
        for m in range(n_x):
            team_mine[j, m, 0:16, :] = grad[16 * m:16 * (m + 1), :]
            team_mine[j, m, 16:17, :] = bias_grad
    back_sends = []
    for k in range(1, n_rep):
        c = send(back_mine.at[(rep + k) % n_rep], back.at[rep], ss_back.at[k - 1], rs_back.at[k - 1], rep_at(k))
        c.start()
        back_sends.append(c)
    back[rep] = back_mine[rep]
    for n, (k, m) in enumerate(team):
        c = send(
            team_mine.at[(rep + k) % n_rep, (chip + m) % n_x, 0:17], team_in.at[rep, chip, 0:17],
            ss_team.at[n], rs_team.at[n], team_at(k, m),
        )
        c.start()
        team_sends.append(c)
    team_in[rep, chip, 0:17] = team_mine[rep, chip, 0:17]
    for n, k in enumerate(back_order):
        if k:
            back_sends[n_rep - k - 1].wait_recv()

        @pl.loop(0, per, unroll=True)
        def _(q, n=n, k=k):
            chunk = (rep + k) % n_rep
            lhs = back[chunk, q]
            for s in range(0, n_slot, BACK_GROUP):
                some = dot(lhs, join([tiles[chunk * per + q, s + t] for t in range(BACK_GROUP)]), NN)
                for u in range(BACK_GROUP):
                    t = (n * per + q) * n_slot + s + u
                    run[t] = some[:, u * TILE:(u + 1) * TILE] + run[table_s[1, t]]

    for c in team_sends:
        c.wait_recv()
    s3_mine[0:17, :] = sum(team_in[k, m, 0:17] for k in range(n_rep) for m in range(n_x))
    s3_sends = []
    for n, o in enumerate(column):
        c = send(s3_mine.at[0:17], s3_in.at[layer, core, 0:17], ss_s3.at[n], rs_s3.at[n], column_at(*o))
        c.start()
        s3_sends.append(c)
    part_sends = {}
    for g in feat_order:
        for b in range(n_blk):
            part[g, b] = run[table_s[2, g * n_blk + b]].astype(BF16)
        part_sends[g] = send(
            part.at[g], part_in.at[g], ss_part.at[g], rs_part.at[g], row_at(offsets[g])
        )
        part_sends[g].start()

    s3_in[layer, core, 0:17] = s3_mine[0:17, :]
    for k in range(1, n_rep):
        c = send(hid_mine.at[(rep + k) % n_rep], hid_out.at[:, mine], ss_hid.at[k - 1], rs_hid.at[k - 1], rep_at(k))
        c.start()
        hid_sends.append(c)
    keep_hid = pltpu.make_async_copy(hid_mine.at[rep], hid_out.at[:, mine], sem_local.at[3])
    keep_hid.start()

    for c in s3_sends:
        c.wait_recv()
    done = sum(s3_in[m, c, 0:17] for m in range(depth) for c in range(2))
    gw_mine[...] = done[0:16, :]
    gb_mine[...] = jnp.broadcast_to(done[16:17, :], gb_mine.shape)
    keep_gb = pltpu.make_async_copy(gb_mine, gb_out, sem_local.at[5])
    keep_gb.start()
    my_rows = pl.ds(pl.multiple_of(chip * 16, 16), 16)
    s4_sends = []
    for k in chips:
        c = send(gw_mine, gw_out.at[my_rows, :], ss_s4.at[k - 1], rs_s4.at[k - 1], team_at(0, k))
        c.start()
        s4_sends.append(c)
    keep_gw = pltpu.make_async_copy(gw_mine, gw_out.at[my_rows, :], sem_local.at[4])
    keep_gw.start()

    for g in far_first:
        part_sends[g].wait_recv()
    for b in range(n_blk):
        value = run[table_s[2, OWN * n_blk + b]]
        for g in far_first:
            value += part_in[g, b].astype(F32)
        gf_mine[:, b * TILE:(b + 1) * TILE] = value.astype(BF16)
    keep_gf = pltpu.make_async_copy(gf_mine, gf_out, sem_local.at[2])
    keep_gf.start()

    for c in hid_sends + s4_sends:
        c.wait_recv()
    keep_hid.wait()
    keep_gw.wait()
    keep_gb.wait()
    keep_gf.wait()
    everything = [feat_sends[g] for g in far_first] + pre_sends + agg_sends + back_sends + hid_sends
    everything += team_sends + s3_sends + s4_sends + [part_sends[g] for g in far_first]
    for c in everything:
        c.wait_send()


def finish(hid_in, gw_in, gb_in, gf_in, hid_out, gw_out, gb_out, gf_out, hid, gw, gb, gf, sems):
    through = ((hid_in, hid, hid_out), (gf_in, gf, gf_out), (gw_in, gw, gw_out))
    loads = [pltpu.make_async_copy(a, b, sems.at[0, n]) for n, (a, b, c) in enumerate(through)]
    loads.append(pltpu.make_async_copy(gb_in, gb, sems.at[0, 3]))
    stores = [pltpu.make_async_copy(b, c, sems.at[1, n]) for n, (a, b, c) in enumerate(through)]
    for c in loads:
        c.start()
    for n, c in enumerate(stores):
        loads[n].wait()
        c.start()
    loads[3].wait()
    gb_out[...] = gb[0:1, 0:gb_out.shape[1]]
    for c in stores:
        c.wait()


def body(n_row, n_rep, plane, features, tiles, tile_cols, counts, weight, bias, cotangent):
    n_blk, n_slot = tiles.shape[:2]
    rows, width = features.shape
    n_hid = weight.shape[1]
    fin = weight.shape[0]
    span = rows // n_rep
    depth = n_row // plane
    n_far = len(OFFSETS)
    n_slots = n_blk * n_slot
    dma = pltpu.SemaphoreType.DMA
    vmem = pl.BlockSpec(memory_space=pltpu.VMEM)
    smem = pl.BlockSpec(memory_space=pltpu.SMEM)
    hbm = pl.BlockSpec(memory_space=pltpu.HBM)

    def pair(*shape):
        return [dma(shape), dma(shape)]

    out = pl.pallas_call(
        functools.partial(kernel, n_row, n_rep, plane),
        out_shape=(
            jax.ShapeDtypeStruct((n_hid, rows), BF16),
            jax.ShapeDtypeStruct((n_hid, fin), F32),
            jax.ShapeDtypeStruct((8, TILE), F32),
            jax.ShapeDtypeStruct((width, rows), BF16),
        ),
        in_specs=[hbm] * 7,
        out_specs=(hbm, hbm, hbm, hbm),
        scratch_shapes=[
            pltpu.VMEM(tile_cols.shape, jnp.int32),
            pltpu.SMEM(counts.shape, jnp.int32),
            pltpu.VMEM((1, n_hid), F32),
            pltpu.VMEM(tiles.shape, BF16),
            pltpu.VMEM((len(OFFSETS) * n_blk + 1, width, TILE), BF16),
            pltpu.VMEM((n_rep, n_hid, span), BF16),
            pltpu.VMEM((n_rep, n_hid, fin), BF16),
            pltpu.VMEM((n_rep, 8, TILE), F32),
            pltpu.VMEM((fin, n_rep * n_hid), BF16),
            pltpu.VMEM((n_rep, n_hid, TILE), F32),
            pltpu.VMEM((n_blk, TILE), jnp.int32),
            pltpu.VMEM((8, TILE), jnp.int32),
            pltpu.SMEM((8, TILE), jnp.int32),
            pltpu.VMEM((n_rep, n_blk // n_rep, width, TILE), BF16),
            pltpu.VMEM((n_rep, n_blk // n_rep, width, TILE), BF16),
            pltpu.VMEM((n_rep, n_hid, span), BF16),
            pltpu.VMEM((n_rep, n_hid, span), BF16),
            pltpu.VMEM((n_rep, n_blk // n_rep, width, TILE), BF16),
            pltpu.VMEM((n_rep, n_blk // n_rep, width, TILE), BF16),
            pltpu.VMEM((n_slots + 1, width, TILE), F32),
            pltpu.VMEM((n_far, n_blk, width, TILE), BF16),
            pltpu.VMEM((n_far, n_blk, width, TILE), BF16),
            pltpu.VMEM((n_rep, plane // 2, 24, TILE), F32),
            pltpu.VMEM((n_rep, plane // 2, 24, TILE), F32),
            pltpu.VMEM((24, TILE), F32),
            pltpu.VMEM((depth, 2, 24, TILE), F32),
            pltpu.VMEM((16, TILE), F32),
            pltpu.VMEM((8, TILE), F32),
            pltpu.VMEM((width, rows), BF16),
            dma((n_blk,)),
            dma((n_rep,)),
            dma((8,)),
            *pair(n_far),
            *pair(3, n_rep - 1),
            *pair(n_rep - 1),
            *pair(n_rep - 1),
            *pair(n_rep - 1),
            *pair(n_rep * plane // 2 - 1),
            *pair(depth * 2 - 1),
            *pair(plane // 2 - 1),
            *pair(n_far),
        ],
        compiler_params=pltpu.CompilerParams(
            collective_id=0, has_side_effects=True, vmem_limit_bytes=62 * 1024 * 1024
        ),
        cost_estimate=pl.CostEstimate(
            flops=4 * n_slots * TILE * TILE * width, bytes_accessed=tiles.size * 2, transcendentals=span * n_rep * n_hid
        ),
    )(
        tile_cols, counts, bias.reshape(1, n_hid), features.T, tiles, weight.T, cotangent.T,
    )
    hidden, grad_weight, grad_bias, grad_features = pl.pallas_call(
        finish,
        out_shape=(
            jax.ShapeDtypeStruct((n_hid, rows), BF16),
            jax.ShapeDtypeStruct((n_hid, fin), F32),
            jax.ShapeDtypeStruct((1, n_hid), F32),
            jax.ShapeDtypeStruct((width, rows), BF16),
        ),
        in_specs=[hbm] * 4,
        out_specs=(hbm, hbm, vmem, hbm),
        scratch_shapes=[
            pltpu.VMEM((n_hid, rows), BF16),
            pltpu.VMEM((n_hid, fin), F32),
            pltpu.VMEM((8, TILE), F32),
            pltpu.VMEM((width, rows), BF16),
            dma((2, 4)),
        ],
        compiler_params=pltpu.CompilerParams(vmem_limit_bytes=62 * 1024 * 1024),
    )(*out)
    return hidden.T, grad_weight.T, grad_bias.reshape(n_hid), grad_features.T


def solution(mesh):
    in_specs = (
        P("row", "rep"),
        P("row", None, None, None),
        P("row", None),
        P("row"),
        P(None, "rep"),
        P("rep"),
        P("row", "rep"),
    )
    out_specs = (P("row", "rep"), P(None, "rep"), P("rep"), P("row", "rep"))
    n_row, n_rep = mesh.shape["row"], mesh.shape["rep"]
    step = functools.partial(body, n_row, n_rep, 8)
    return jax.shard_map(step, mesh=mesh, in_specs=in_specs, out_specs=out_specs, check_vma=False)
```
